128 devices in a mesh: items: 32 (over z, x, core), book: 4 (over y).
Axes of the slice: x: 4, y: 4, z: 4, core: 2. Of those that a mesh axis runs over, the one named last changes fastest.
Arguments:
- hidden: bfloat16 [32768, 768], P(('items', 'book')), may hold values from -24 to 24
- enc_weight: bfloat16 [768, 768], replicated, may hold values from -0.21875 to 0.21875
- codebook: bfloat16 [3, 8192, 768], P(None, 'book'), may hold values from -4 to 4
- codes: int32 [3, 32768], P(None, ('items', 'book')), may hold values from 0 to 8191, as said below
Outputs:
- code_grad: float32 [3, 4, 2048, 768], P(None, 'book', 'items')
- enc_grad: float32 [768, 768], replicated
- last_residual: float32 [32768, 768], P(('items', 'book'))
The draws below stay inside these ranges and needn't reach their ends.
Inputs may be any that keep to these rules, and one draw needn't show every extreme that they name: At every level, among the 256 items of one device (aligned blocks of 256 items) at most 128 have a code in any one block of 2048 consecutive codes, and in every block and level one such code block holds exactly 128 of them.
All inputs are finite; a program needn't handle non-finite values.
Results may differ from the reference program's by a relative error of at most 0.0019.
Values may be sent and summed in bfloat16 or wider, within the bound.
A program may use at most 128 MiB of HBM per device.

```python
import jax
import jax.numpy as jnp

D = 768
CODES = 8192
LEVELS = 3
TOK_DEV = 256
ITEMS = 32768
N_BOOK = 4


def draw_codes(key, part):
    key = jax.random.fold_in(key, 11)
    keys = jax.random.split(key, 7)
    blocks = ITEMS // TOK_DEV
    half_dev = TOK_DEV // 2
    span = CODES // N_BOOK
    first = jax.random.randint(keys[0], (LEVELS, blocks, 1), 0, N_BOOK)
    other = (first + 1 + jax.random.randint(keys[1], (LEVELS, blocks, TOK_DEV), 0, N_BOOK - 1)) % N_BOOK
    places = jnp.arange(TOK_DEV, dtype=jnp.int32)[None, None, :]
    shard = jnp.where(places < half_dev, first, other)
    order_keys = jax.random.split(keys[2], LEVELS * blocks)
    order = jax.vmap(lambda k: jax.random.permutation(k, TOK_DEV))(order_keys).reshape(LEVELS, blocks, TOK_DEV)
    shard = jnp.take_along_axis(shard, order, axis=2)
    first_u = jax.random.randint(keys[3], (LEVELS, blocks, TOK_DEV), 0, span)
    second_u = jax.random.randint(keys[4], (LEVELS, blocks, TOK_DEV), 0, span)
    third_u = jax.random.randint(keys[5], (LEVELS, blocks, TOK_DEV), 0, span)
    inner = (first_u * second_u + third_u) // span
    rotate = jax.random.randint(keys[6], (LEVELS, 1, 1), 0, span)
    inner = (inner + rotate) % span
    return (shard * span + inner).reshape(LEVELS, ITEMS).astype(jnp.int32)


def raised(drawn, own_key, source, target, parts, factor):
    owner, partner = [(jnp.arange(drawn.shape[axis_at]) // (drawn.shape[axis_at] // parts)).reshape([-1 if axis == axis_at else 1 for axis in range(drawn.ndim)]) for axis_at in (source, target)]
    chosen = jax.random.permutation(own_key, parts)[partner]
    strong = (owner == chosen) | (owner == (partner + parts // 2) % parts)
    return jnp.where(strong, factor * drawn, drawn)


def steps_of(stream_key, shape, cuts, low, top_value):
    level = 1.0
    for position, shards_of in cuts:
        steps = jax.random.uniform(jax.random.fold_in(jax.random.fold_in(stream_key, 6), position), (shards_of,), jnp.float32, low / len(cuts), top_value / len(cuts))
        level = level * jnp.repeat(jnp.exp(steps), shape[position] // shards_of).reshape((-1,) + (1,) * (len(shape) - 1 - position))
    return level


def normal_values(rng, extent, spread, bound, cuts=(), kind=jnp.bfloat16):
    entries = spread * jax.random.normal(rng, extent, jnp.float32)
    if cuts:
        entries = entries * steps_of(rng, extent, cuts, -0.22, 0.18)
    return jnp.clip(entries, -bound, bound).astype(kind)


def gaussian_with(own_key, dims, deviation, limit, pieces, heavy, kind=jnp.bfloat16):
    result = deviation * jax.random.normal(own_key, dims, jnp.float32)
    if pieces:
        result = result * steps_of(own_key, dims, pieces, -0.22, 0.18)
    return jnp.clip(raised(result, jax.random.fold_in(own_key, 3), *heavy), -limit, limit).astype(kind)


def setup_inputs(seed: int = 0) -> dict:
    seeds = jax.random.split(jax.random.key(seed), 5)
    hidden = gaussian_with(seeds[0], (ITEMS, D), 1.0, 24.0, ((0, 128),), (0, 1, 128, 5.5))
    enc_weight = normal_values(seeds[1], (D, D), D ** -0.5, 0.21875)
    codebook = normal_values(seeds[2], (LEVELS, CODES, D), 0.6, 4.0, ((1, 4),))
    codes = draw_codes(jax.random.fold_in(seeds[4], 71), 0)
    return {"hidden": hidden, "enc_weight": enc_weight, "codebook": codebook, "codes": codes}


def reference(hidden, enc_weight, codebook, codes):
    lifted = jnp.dot(hidden, enc_weight, preferred_element_type=jnp.float32)
    residual = lifted
    history = []
    for level in range(LEVELS):
        fetched = jnp.take(codebook[level], codes[level], axis=0).astype(jnp.float32)
        residual = residual - fetched
        history.append(residual)
    carried = jnp.zeros(lifted.shape, jnp.float32)
    grads = [None] * LEVELS
    for level in reversed(range(LEVELS)):
        carried = carried + history[level]
        grads[level] = carried.astype(jnp.bfloat16)
    enc_grad = jnp.dot(hidden.T, grads[0], preferred_element_type=jnp.float32) / ITEMS
    tables = []
    for level in range(LEVELS):
        summed = jax.ops.segment_sum(grads[level].astype(jnp.float32), codes[level], num_segments=CODES)
        tables.append(-summed)
    code_grad = jnp.stack(tables).reshape(LEVELS, N_BOOK, CODES // N_BOOK, D)
    return code_grad, enc_grad, history[-1]
```

```python
import jax
import jax.numpy as jnp
from jax import lax
from jax.experimental import pallas as pl
from jax.experimental.pallas import tpu as pltpu
from jax.sharding import PartitionSpec as P

MESH = pl.DeviceIdType.MESH
F32 = jnp.float32
BF16 = jnp.bfloat16
I32 = jnp.int32

TOK = 256
D = 768
LEVELS = 3
SHARD = 2048
CAP = 128
SLOTS = 4 * CAP
CW = 256
NCH = D // CW


def onehot(mask):
    return jnp.where(mask, 1.0, 0.0).astype(BF16)


def dot(a, b):
    return jnp.dot(a, b, preferred_element_type=F32)


def iota(shape, axis):
    return lax.broadcasted_iota(I32, shape, axis)


def kernel(
    hid, w, cb_hbm, codes, cg_out, enc_out, res_out,
    cb, code8, pk, rc, rcs, ut, u, oh, fs, rr, gs, gr, gsib, dd,
    s1s, s1r, s2s, s2r, e, ec, e1r, e2s, e2r, ey,
    cb_sem, pk_ss, pk_rs, rcs_ss, rcs_rs, f_ss, f_rs, g_ss, g_rs, sib_ss, sib_rs,
    s1_ss, s1_rs, s2_ss, s2_rs, ec_ss, ec_rs, e1_ss, e1_rs, e2_ss, e2_rs, ey_ss, ey_rs,
    a1_ss, a1_rs, a2_ss, a2_rs, a3_ss, a3_rs,
):
    i = lax.axis_index("items")
    y = lax.axis_index("book")
    c = i % 2
    x = (i // 2) % 4
    z = i // 8

    def at_y(k):
        return (i, (y + k) % 4)

    def at_x(k):
        return (z * 8 + ((x + k) % 4) * 2 + c, y)

    def at_z(k):
        return (((z + k) % 4) * 8 + x * 2 + c, y)

    sib = (z * 8 + x * 2 + (1 - c), y)

    def remote(src, dst, ss, rs, dev):
        return pltpu.make_async_remote_copy(
            src_ref=src, dst_ref=dst, send_sem=ss, recv_sem=rs, device_id=dev, device_id_type=MESH
        )

    cb_cp = [pltpu.make_async_copy(cb_hbm.at[l], cb.at[l], cb_sem.at[l]) for l in range(LEVELS)]
    for cp in cb_cp:
        cp.start()
    bar = pltpu.get_barrier_semaphore()
    for k in (1, 2, 3):
        pl.semaphore_signal(bar, inc=1, device_id=at_y(k), device_id_type=MESH)
        pl.semaphore_signal(bar, inc=1, device_id=at_x(k), device_id_type=MESH)
        pl.semaphore_signal(bar, inc=1, device_id=at_z(k), device_id_type=MESH)
    pl.semaphore_signal(bar, inc=1, device_id=sib, device_id_type=MESH)

    code8[...] = jnp.zeros_like(code8)
    code8[0:LEVELS, :] = codes[...]
    cv = code8[...]
    dist = ((cv >> 11) - y) & 3
    val = (cv & (SHARD - 1)) + 1
    tri = onehot(iota((TOK, TOK), 0) < iota((TOK, TOK), 1))
    pos = jnp.zeros((8, TOK), F32)
    for k in range(4):
        m = jnp.where(dist == k, 1.0, 0.0)
        pos = pos + m * (k * CAP + dot(m.astype(BF16), tri))
    pos_i = pos.astype(I32)
    pos_t = pos.T.astype(I32)
    hl = jnp.concatenate([(val >> 6).astype(F32), (val & 63).astype(F32)], axis=0).astype(BF16)
    pk[...] = jnp.zeros_like(pk)
    for l in range(LEVELS):
        ut[l] = onehot(iota((SLOTS, TOK), 0) == pos_i[l : l + 1, :])
        ul = onehot(iota((TOK, SLOTS), 1) == pos_t[:, l : l + 1])
        u[l] = ul
        pc = dot(hl, ul)
        row = pc[l : l + 1, :] * 64.0 + pc[8 + l : 9 + l, :]
        for k in range(4):
            pk[k, l : l + 1, :] = row[:, k * CAP : (k + 1) * CAP]
    rc[0] = pk[0]

    pl.semaphore_wait(bar, 10)
    pk_cp = [
        remote(pk.at[k], rc.at[4 - k], pk_ss.at[k - 1], pk_rs.at[k - 1], at_y(k)) for k in (1, 2, 3)
    ]
    for cp in pk_cp:
        cp.start()
    for cp in pk_cp:
        cp.wait()
    rcs_cp = remote(rc, rcs, rcs_ss, rcs_rs, sib)
    rcs_cp.start()

    held = jnp.concatenate([rc[k] for k in range(4)], axis=1)
    held_t = held.T.astype(I32)

    for l in range(LEVELS):
        col = held_t[:, l : l + 1]
        for h in range(2):
            oh[l, h * SLOTS : (h + 1) * SLOTS, :] = onehot(
                iota((SLOTS, 1024), 1) + (1 + h * 1024) == col
            )
    for cp in cb_cp:
        cp.wait()

    f_cp = []
    for ch in range(NCH):
        cols = slice(ch * CW, (ch + 1) * CW)

        def fetch(l, _, ch=ch, cols=cols):
            got = dot(oh[l, 0:SLOTS, :], cb[l, 0:1024, cols])
            got = got + dot(oh[l, SLOTS:, :], cb[l, 1024:2048, cols])
            got = got.astype(BF16)
            rr[ch, 0, l] = got[0:CAP]
            for k in (1, 2, 3):
                fs[ch, k - 1, l] = got[k * CAP : (k + 1) * CAP]
            return 0

        lax.fori_loop(0, LEVELS, fetch, 0)
        f_cp.append([
            remote(fs.at[ch, k - 1], rr.at[ch, 4 - k], f_ss.at[ch, k - 1], f_rs.at[ch, k - 1], at_y(k))
            for k in (2, 1, 3)
        ])
        if ch < 2:
            for cp in f_cp[ch]:
                cp.start()

    g_cp = []

    def chain(ch):
        cols = slice(ch * CW, (ch + 1) * CW)
        lifted = dot(hid[...], w[:, cols])
        res = []
        r = lifted
        for l in range(LEVELS):
            r = r - dot(u[l], rr[ch, :, l].reshape(SLOTS, CW))
            res.append(r)
        res_out[:, cols] = r
        carried = jnp.zeros_like(r)
        for l in reversed(range(LEVELS)):
            carried = carried + res[l]
            cl = carried.astype(BF16)
            packed = dot(ut[l], cl).astype(BF16)
            gr[ch, 0, l] = packed[0:CAP]
            for k in (1, 2, 3):
                gs[ch, k - 1, l] = packed[k * CAP : (k + 1) * CAP]
            if l == 0:
                prod = lax.dot_general(
                    hid[...], cl, (((0,), (0,)), ((), ())), preferred_element_type=F32
                )
                e[:, :, :, :, cols] = prod.reshape(2, 4, 4, 24, CW)
        cps = [
            remote(gs.at[ch, k - 1], gr.at[ch, 4 - k], g_ss.at[ch, k - 1], g_rs.at[ch, k - 1], at_y(k))
            for k in (2, 1, 3)
        ]
        for cp in cps:
            cp.start()
        g_cp.append(cps)

    for cp in f_cp[0]:
        cp.wait()
    chain(0)
    for cp in f_cp[1]:
        cp.wait()
    for cp in f_cp[2]:
        cp.start()
    chain(1)

    rcs_cp.wait()
    for l in range(LEVELS):
        for h, src in enumerate((rc, rcs)):
            slot_code = jnp.concatenate(
                [src[k, l : l + 1, :] for k in range(4)], axis=1
            ).astype(I32)
            rows = iota((1024, SLOTS), 0)
            code = ((rows >> 6) << 7) + c * 64 + (rows & 63) + 1
            oh[l, :, h * SLOTS : (h + 1) * SLOTS] = onehot(code == slot_code)

    for cp in g_cp[0]:
        cp.wait()
    sib_cp = []

    def to_sib(ch):
        cp = remote(gr.at[ch], gsib.at[ch], sib_ss.at[ch], sib_rs.at[ch], sib)
        cp.start()
        sib_cp.append(cp)

    to_sib(0)

    for cp in f_cp[2]:
        cp.wait()
    chain(2)
    ec_cp = remote(e.at[1 - c], ec, ec_ss, ec_rs, sib)
    ec_cp.start()

    s1_cp = []

    def stage1(ch):
        sib_cp[ch].wait()

        def dense(l, _):
            acc = dot(oh[l, :, 0:SLOTS], gr[ch, :, l].reshape(SLOTS, CW))
            acc = acc + dot(oh[l, :, SLOTS:], gsib[ch, :, l].reshape(SLOTS, CW))
            dd[ch % 2, l] = acc.reshape(4, 4, 64, CW)
            for k in (1, 2, 3):
                s1s[ch, 0, k - 1, l] = dd[ch % 2, l, :, (x + k) % 4, 0:32, :].astype(BF16)
                s1s[ch, 1, k - 1, l] = dd[ch % 2, l, (z + k) % 4, :, 32:64, :].astype(BF16)
            return 0

        lax.fori_loop(0, LEVELS, dense, 0)
        cps = []
        for k in (2, 1, 3):
            for h, at in enumerate((at_x, at_z)):
                cps.append(remote(
                    s1s.at[ch, h, k - 1], s1r.at[ch, h, k - 1],
                    s1_ss.at[ch, h, k - 1], s1_rs.at[ch, h, k - 1], at(k),
                ))
        for cp in cps:
            cp.start()
        s1_cp.append(cps)

    s2_cp = []

    def stage2(ch):
        for cp in s1_cp[ch]:
            cp.wait()

        def sums(l, _):
            tx = dd[ch % 2, l, :, x, 0:32, :]
            tz = dd[ch % 2, l, z, :, 32:64, :]
            for k in range(3):
                tx = tx + s1r[ch, 0, k, l].astype(F32)
                tz = tz + s1r[ch, 1, k, l].astype(F32)
            s2s[ch, 0, :, l] = tx
            s2s[ch, 1, :, l] = tz
            return 0

        lax.fori_loop(0, LEVELS, sums, 0)
        cps = []
        for k in (2, 1, 3):
            cps.append(remote(
                s2s.at[ch, 0, (z + k) % 4], s2r.at[ch, 0, k - 1],
                s2_ss.at[ch, 0, k - 1], s2_rs.at[ch, 0, k - 1], at_z(k),
            ))
            cps.append(remote(
                s2s.at[ch, 1, (x + k) % 4], s2r.at[ch, 1, k - 1],
                s2_ss.at[ch, 1, k - 1], s2_rs.at[ch, 1, k - 1], at_x(k),
            ))
        for cp in cps:
            cp.start()
        s2_cp.append(cps)

    def finish(ch):
        cols = slice(ch * CW, (ch + 1) * CW)
        for cp in s2_cp[ch]:
            cp.wait()
        t0 = s2s[ch, 0, z]
        t1 = s2s[ch, 1, x]
        for k in range(3):
            t0 = t0 + s2r[ch, 0, k]
            t1 = t1 + s2r[ch, 1, k]
        cg_out[:, 0:32, cols] = -t0
        cg_out[:, 32:64, cols] = -t1

    stage1(0)

    ec_cp.wait()
    e[c] = e[c] + ec[...]
    H = D // 2
    e1_cp = []
    for k in (2, 1, 3):
        e1_cp.append(remote(
            e.at[c, :, (x + k) % 4, :, 0:H], e1r.at[0, k - 1],
            e1_ss.at[0, k - 1], e1_rs.at[0, k - 1], at_x(k),
        ))
        e1_cp.append(remote(
            e.at[c, (z + k) % 4, :, :, H:D], e1r.at[1, k - 1],
            e1_ss.at[1, k - 1], e1_rs.at[1, k - 1], at_z(k),
        ))
    for cp in e1_cp:
        cp.start()

    for cp in g_cp[1]:
        cp.wait()
    to_sib(1)
    stage2(0)
    stage1(1)

    for cp in e1_cp:
        cp.wait()
    t0 = e[c, :, x, :, 0:H]
    t1 = e[c, z, :, :, H:D]
    for k in range(3):
        t0 = t0 + e1r[0, k]
        t1 = t1 + e1r[1, k]
    e2s[0] = t0
    e2s[1] = t1
    e2_cp = []
    for k in (2, 1, 3):
        e2_cp.append(remote(
            e2s.at[0, (z + k) % 4], e2r.at[0, k - 1], e2_ss.at[0, k - 1], e2_rs.at[0, k - 1], at_z(k)
        ))
        e2_cp.append(remote(
            e2s.at[1, (x + k) % 4], e2r.at[1, k - 1], e2_ss.at[1, k - 1], e2_rs.at[1, k - 1], at_x(k)
        ))
    for cp in e2_cp:
        cp.start()
    for cp in g_cp[2]:
        cp.wait()
    to_sib(2)
    finish(0)
    for cp in e2_cp:
        cp.wait()
    t0 = e2s[0, z]
    t1 = e2s[1, x]
    for k in range(3):
        t0 = t0 + e2r[0, k]
        t1 = t1 + e2r[1, k]
    ey[y, :, 0:H] = t0
    ey[y, :, H:D] = t1
    ey_cp = [
        remote(ey.at[y], ey.at[y], ey_ss.at[k - 1], ey_rs.at[k - 1], at_y(k)) for k in (2, 1, 3)
    ]
    for cp in ey_cp:
        cp.start()
    stage2(1)
    stage1(2)
    for cp in ey_cp:
        cp.wait()
    enc_out[c, z, x] = (((ey[0] + ey[1]) + ey[2]) + ey[3]) * (1.0 / (TOK * 128))

    def gather(step, ss, rs):
        cps = []
        for k in (2, 1, 3):
            if step == 1:
                va = enc_out.at[c, z, x, :, 0:H]
                vb = enc_out.at[c, z, x, :, H:D]
                da, db = at_x(k), at_z(k)
            else:
                va = enc_out.at[c, z, :, :, 0:H]
                vb = enc_out.at[c, :, x, :, H:D]
                da, db = at_z(k), at_x(k)
            cps.append(remote(va, va, ss.at[0, k - 1], rs.at[0, k - 1], da))
            cps.append(remote(vb, vb, ss.at[1, k - 1], rs.at[1, k - 1], db))
        for cp in cps:
            cp.start()
        return cps

    a1_cp = gather(1, a1_ss, a1_rs)
    finish(1)
    for cp in a1_cp:
        cp.wait()
    a2_cp = gather(2, a2_ss, a2_rs)
    stage2(2)
    for cp in a2_cp:
        cp.wait()
    a3_cp = remote(enc_out.at[c], enc_out.at[c], a3_ss, a3_rs, sib)
    a3_cp.start()
    finish(2)
    a3_cp.wait()


def on_device(hidden, enc_weight, codebook, codes):
    dma = pltpu.SemaphoreType.DMA
    vmem = pltpu.VMEM
    H = D // 2
    scratch = [
        vmem((LEVELS, SHARD, D), BF16),
        vmem((8, TOK), I32),
        vmem((4, 8, CAP), F32),
        vmem((4, 8, CAP), F32),
        vmem((4, 8, CAP), F32),
        vmem((LEVELS, SLOTS, TOK), BF16),
        vmem((LEVELS, TOK, SLOTS), BF16),
        vmem((LEVELS, 1024, 1024), BF16),
        vmem((NCH, 3, LEVELS, CAP, CW), BF16),
        vmem((NCH, 4, LEVELS, CAP, CW), BF16),
        vmem((NCH, 3, LEVELS, CAP, CW), BF16),
        vmem((NCH, 4, LEVELS, CAP, CW), BF16),
        vmem((NCH, 4, LEVELS, CAP, CW), BF16),
        vmem((2, LEVELS, 4, 4, 64, CW), F32),
        vmem((NCH, 2, 3, LEVELS, 4, 32, CW), BF16),
        vmem((NCH, 2, 3, LEVELS, 4, 32, CW), BF16),
        vmem((NCH, 2, 4, LEVELS, 32, CW), F32),
        vmem((NCH, 2, 3, LEVELS, 32, CW), F32),
        vmem((2, 4, 4, 24, D), F32),
        vmem((4, 4, 24, D), F32),
        vmem((2, 3, 4, 24, H), F32),
        vmem((2, 4, 24, H), F32),
        vmem((2, 3, 24, H), F32),
        vmem((4, 24, D), F32),
        dma((LEVELS,)),
        dma((3,)), dma((3,)), dma, dma,
        dma((NCH, 3)), dma((NCH, 3)), dma((NCH, 3)), dma((NCH, 3)),
        dma((NCH,)), dma((NCH,)),
        dma((NCH, 2, 3)), dma((NCH, 2, 3)), dma((NCH, 2, 3)), dma((NCH, 2, 3)),
        dma, dma,
        dma((2, 3)), dma((2, 3)), dma((2, 3)), dma((2, 3)),
        dma((3,)), dma((3,)),
        dma((2, 3)), dma((2, 3)), dma((2, 3)), dma((2, 3)),
        dma, dma,
    ]
    in_vmem = pl.BlockSpec(memory_space=pltpu.VMEM)
    code_grad, enc_grad, last = pl.pallas_call(
        kernel,
        out_shape=(
            jax.ShapeDtypeStruct((LEVELS, 64, D), F32),
            jax.ShapeDtypeStruct((2, 4, 4, 24, D), F32),
            jax.ShapeDtypeStruct((TOK, D), F32),
        ),
        in_specs=[in_vmem, in_vmem, pl.BlockSpec(memory_space=pl.ANY), in_vmem],
        out_specs=(in_vmem, in_vmem, in_vmem),
        scratch_shapes=scratch,
        compiler_params=pltpu.CompilerParams(
            collective_id=0, has_side_effects=True, vmem_limit_bytes=62 * 2**20
        ),
        cost_estimate=pl.CostEstimate(flops=13 * 10**9, bytes_accessed=16 * 10**6, transcendentals=0),
        name="quantizer_step",
    )(hidden, enc_weight, codebook, codes)
    return code_grad[:, None], enc_grad.reshape(D, D), last


def solution(mesh):
    in_specs = (P(("items", "book"), None), P(), P(None, "book", None), P(None, ("items", "book")))
    out_specs = (P(None, "book", "items", None), P(), P(("items", "book"), None))
    return jax.shard_map(
        on_device, mesh=mesh, in_specs=in_specs, out_specs=out_specs, check_vma=False
    )
```

```python
import jax
import jax.numpy as jnp
from jax import lax
from jax.experimental import pallas as pl
from jax.experimental.pallas import tpu as pltpu
from jax.sharding import PartitionSpec as P

MESH = pl.DeviceIdType.MESH
F32 = jnp.float32
BF16 = jnp.bfloat16
I32 = jnp.int32

TOK = 256
D = 768
LEVELS = 3
SHARD = 2048
CAP = 128
SLOTS = 4 * CAP
CW = 256
NCH = D // CW
UNITS = [(ch, l) for ch in range(NCH) for l in (2, 1, 0)]
RING = 6


def onehot(mask):
    return jnp.where(mask, 1.0, 0.0).astype(BF16)


def dot(a, b):
    return jnp.dot(a, b, preferred_element_type=F32)


def iota(shape, axis):
    return lax.broadcasted_iota(I32, shape, axis)


def kernel(
    hid_hbm, w_hbm, cb_hbm, codes, cg_hbm, enc_hbm, res_hbm,
    hid, w, cb, code8, pk, rc, rcs, ut, u, oh, fs, rr, gs, gr, gsib, dd,
    fars, farr, nears, nearr, s2s, s2r, e, ec, e1r, e2s, e2r, ey, cg_out, enc_out, res_out,
    in_sem, cb_sem, out_sem, pk_ss, pk_rs, rcs_ss, rcs_rs, f_ss, f_rs, g_ss, g_rs, sib_ss, sib_rs,
    far_ss, far_rs, near_ss, near_rs, s2_ss, s2_rs, ec_ss, ec_rs, e1_ss, e1_rs, e2_ss, e2_rs,
    ey_ss, ey_rs, a1_ss, a1_rs, a2_ss, a2_rs, a3_ss, a3_rs,
):
    i = lax.axis_index("items")
    y = lax.axis_index("book")
    c = i % 2
    x = (i // 2) % 4
    z = i // 8

    def at_y(k):
        return (i, (y + k) % 4)

    def at_x(k):
        return (z * 8 + ((x + k) % 4) * 2 + c, y)

    def at_z(k):
        return (((z + k) % 4) * 8 + x * 2 + c, y)

    sib = (z * 8 + x * 2 + (1 - c), y)

    def remote(src, dst, ss, rs, dev):
        return pltpu.make_async_remote_copy(
            src_ref=src, dst_ref=dst, send_sem=ss, recv_sem=rs, device_id=dev, device_id_type=MESH
        )

    def start(cps):
        for cp in cps:
            cp.start()
        return cps

    def wait(cps):
        for cp in cps:
            cp.wait()

    bar = pltpu.get_barrier_semaphore()
    for k in (1, 2, 3):
        pl.semaphore_signal(bar, inc=1, device_id=at_y(k), device_id_type=MESH)
        pl.semaphore_signal(bar, inc=1, device_id=at_x(k), device_id_type=MESH)
        pl.semaphore_signal(bar, inc=1, device_id=at_z(k), device_id_type=MESH)
    pl.semaphore_signal(bar, inc=1, device_id=sib, device_id_type=MESH)
    cb_cp = start([
        pltpu.make_async_copy(cb_hbm.at[l], cb.at[l], cb_sem.at[l]) for l in range(LEVELS)
    ])
    in_cp = start([
        pltpu.make_async_copy(hid_hbm, hid, in_sem.at[0]),
        pltpu.make_async_copy(w_hbm, w, in_sem.at[1]),
    ])

    code8[...] = jnp.zeros_like(code8)
    code8[0:LEVELS, :] = codes[...]
    cv = code8[...]
    dist = ((cv >> 11) - y) & 3
    val = (cv & (SHARD - 1)) + 1
    tri = onehot(iota((TOK, TOK), 0) < iota((TOK, TOK), 1))
    pos = jnp.zeros((8, TOK), F32)
    for k in range(4):
        m = jnp.where(dist == k, 1.0, 0.0)
        pos = pos + m * (k * CAP + dot(m.astype(BF16), tri))
    pos_i = pos.astype(I32)
    pos_t = pos.T.astype(I32)
    hl = jnp.concatenate([(val >> 6).astype(F32), (val & 63).astype(F32)], axis=0).astype(BF16)
    pk[...] = jnp.zeros_like(pk)
    for l in range(LEVELS):
        ul = onehot(iota((TOK, SLOTS), 1) == pos_t[:, l : l + 1])
        u[l] = ul
        pc = dot(hl, ul)
        row = pc[l : l + 1, :] * 64.0 + pc[8 + l : 9 + l, :]
        for k in range(4):
            pk[k, l : l + 1, :] = row[:, k * CAP : (k + 1) * CAP]
    rc[0] = pk[0]

    pl.semaphore_wait(bar, 10)
    pk_cp = start([
        remote(pk.at[k], rc.at[4 - k], pk_ss.at[k - 1], pk_rs.at[k - 1], at_y(k)) for k in (2, 1, 3)
    ])
    for l in range(LEVELS):
        ut[l] = onehot(iota((SLOTS, TOK), 0) == pos_i[l : l + 1, :])
    wait(pk_cp)
    rcs_cp = remote(rc, rcs, rcs_ss, rcs_rs, sib)
    rcs_cp.start()

    held = jnp.concatenate([rc[k] for k in range(4)], axis=1)
    held_t = held.T.astype(I32)

    def fetch_copies(ch, l):
        return [
            remote(
                fs.at[ch, l, k - 1], rr.at[ch, l, 4 - k],
                f_ss.at[ch, l, k - 1], f_rs.at[ch, l, k - 1], at_y(k),
            )
            for k in (2, 1, 3)
        ]

    def fetch(ch, l):
        cols = slice(ch * CW, (ch + 1) * CW)
        got = dot(oh[l, 0:SLOTS, :], cb[l, 0:1024, cols])
        got = got + dot(oh[l, SLOTS:, :], cb[l, 1024:2048, cols])
        got = got.astype(BF16)
        rr[ch, l, 0] = got[0:CAP]
        for k in (1, 2, 3):
            fs[ch, l, k - 1] = got[k * CAP : (k + 1) * CAP]

    f_cp = [[], [], []]
    for l in range(LEVELS):
        col = held_t[:, l : l + 1]
        for h in range(2):
            oh[l, h * SLOTS : (h + 1) * SLOTS, :] = onehot(
                iota((SLOTS, 1024), 1) + (1 + h * 1024) == col
            )
        cb_cp[l].wait()
        fetch(0, l)
        f_cp[0] += start(fetch_copies(0, l))
    for ch in (1, 2):
        for l in range(LEVELS):
            fetch(ch, l)
            f_cp[ch] += fetch_copies(ch, l)
            if ch == 1:
                start(f_cp[1][-3:])
    wait(in_cp)

    g_cp = {}
    ec_cp = {}

    def chain(ch):
        cols = slice(ch * CW, (ch + 1) * CW)
        wait(f_cp[ch])
        r = dot(hid[...], w[:, cols])
        res = []
        for l in range(LEVELS):
            r = r - dot(u[l], rr[ch, l].reshape(SLOTS, CW))
            res.append(r)
        carried = jnp.zeros_like(r)
        for l in reversed(range(LEVELS)):
            carried = carried + res[l]
            cl = carried.astype(BF16)
            packed = dot(ut[l], cl).astype(BF16)
            gr[ch, l, 0] = packed[0:CAP]
            for k in (1, 2, 3):
                gs[ch, l, k - 1] = packed[k * CAP : (k + 1) * CAP]
            g_cp[ch, l] = start([
                remote(
                    gs.at[ch, l, k - 1], gr.at[ch, l, 4 - k],
                    g_ss.at[ch, l, k - 1], g_rs.at[ch, l, k - 1], at_y(k),
                )
                for k in (2, 1, 3)
            ])
        res_out[:, cols] = r
        prod = lax.dot_general(
            hid[...], cl, (((0,), (0,)), ((), ())), preferred_element_type=F32
        )
        e[ch] = prod.reshape(2, 4, 4, 24, CW)
        ec_cp[ch] = start([
            remote(e.at[ch, 1 - c], ec.at[ch], ec_ss.at[ch], ec_rs.at[ch], sib)
        ])

    e1_cp = {}
    e2_cp = {}
    HW = CW // 2

    def enc_b(ch):
        wait(ec_cp[ch])
        e[ch, c] = e[ch, c] + ec[ch]
        cps = []
        for k in (2, 1, 3):
            cps.append(remote(
                e.at[ch, c, :, (x + k) % 4, :, 0:HW], e1r.at[ch, 0, k - 1],
                e1_ss.at[ch, 0, k - 1], e1_rs.at[ch, 0, k - 1], at_x(k),
            ))
            cps.append(remote(
                e.at[ch, c, (z + k) % 4, :, :, HW:CW], e1r.at[ch, 1, k - 1],
                e1_ss.at[ch, 1, k - 1], e1_rs.at[ch, 1, k - 1], at_z(k),
            ))
        e1_cp[ch] = start(cps)

    def enc_c(ch):
        wait(e1_cp[ch])
        t0 = e[ch, c, :, x, :, 0:HW]
        t1 = e[ch, c, z, :, :, HW:CW]
        for k in range(3):
            t0 = t0 + e1r[ch, 0, k]
            t1 = t1 + e1r[ch, 1, k]
        e2s[ch, 0] = t0
        e2s[ch, 1] = t1
        cps = []
        for k in (2, 1, 3):
            cps.append(remote(
                e2s.at[ch, 0, (z + k) % 4], e2r.at[ch, 0, k - 1],
                e2_ss.at[ch, 0, k - 1], e2_rs.at[ch, 0, k - 1], at_z(k),
            ))
            cps.append(remote(
                e2s.at[ch, 1, (x + k) % 4], e2r.at[ch, 1, k - 1],
                e2_ss.at[ch, 1, k - 1], e2_rs.at[ch, 1, k - 1], at_x(k),
            ))
        e2_cp[ch] = start(cps)

    def enc_d(ch):
        wait(e2_cp[ch])
        t0 = e2s[ch, 0, z]
        t1 = e2s[ch, 1, x]
        for k in range(3):
            t0 = t0 + e2r[ch, 0, k]
            t1 = t1 + e2r[ch, 1, k]
        ey[y, :, ch * CW : ch * CW + HW] = t0
        ey[y, :, ch * CW + HW : (ch + 1) * CW] = t1

    sib_cp, far_cp, near_cp, s2_cp, out_cp = {}, {}, {}, {}, []

    def unit_a(n):
        ch, l = UNITS[n]
        wait(g_cp[ch, l])
        sib_cp[n] = start([
            remote(gr.at[ch, l], gsib.at[ch, l], sib_ss.at[ch, l], sib_rs.at[ch, l], sib)
        ])

    def unit_b(n):
        ch, l = UNITS[n]
        q = n % RING
        acc = dot(oh[l, :, 0:SLOTS], gr[ch, l].reshape(SLOTS, CW))
        wait(sib_cp[n])
        acc = acc + dot(oh[l, :, SLOTS:], gsib[ch, l].reshape(SLOTS, CW))
        dd[q] = acc.reshape(4, 4, 64, CW)
        x2 = (x + 2) % 4
        z2 = (z + 2) % 4
        cps = []
        for d, k in enumerate((1, 3)):
            fars[n, 0, d] = dd[q, 2 * d : 2 * d + 2, x2, 0:32, :].astype(BF16)
            fars[n, 1, d] = dd[q, z2, 2 * d : 2 * d + 2, 32:64, :].astype(BF16)
            for h, at in enumerate((at_x, at_z)):
                cps.append(remote(
                    fars.at[n, h, d], farr.at[n, h, d],
                    far_ss.at[n, h, d], far_rs.at[n, h, d], at(k),
                ))
        far_cp[n] = start(cps)

    def unit_c(n):
        q = n % RING
        wait(far_cp[n])
        cps = []
        for d, k in enumerate((1, 3)):
            xk = (x + k) % 4
            zk = (z + k) % 4
            a, b = 2 * d, 2 - 2 * d
            nears[n, 0, d, a : a + 2] = (
                dd[q, a : a + 2, xk, 0:32, :] + farr[n, 0, d].astype(F32)
            ).astype(BF16)
            nears[n, 0, d, b : b + 2] = dd[q, b : b + 2, xk, 0:32, :].astype(BF16)
            nears[n, 1, d, a : a + 2] = (
                dd[q, zk, a : a + 2, 32:64, :] + farr[n, 1, d].astype(F32)
            ).astype(BF16)
            nears[n, 1, d, b : b + 2] = dd[q, zk, b : b + 2, 32:64, :].astype(BF16)
            for h, at in enumerate((at_x, at_z)):
                cps.append(remote(
                    nears.at[n, h, d], nearr.at[n, h, d],
                    near_ss.at[n, h, d], near_rs.at[n, h, d], at(k),
                ))
        near_cp[n] = start(cps)

    def unit_d(n):
        q = n % RING
        wait(near_cp[n])
        tx = dd[q, :, x, 0:32, :]
        tz = dd[q, z, :, 32:64, :]
        for d in range(2):
            tx = tx + nearr[n, 0, d].astype(F32)
            tz = tz + nearr[n, 1, d].astype(F32)
        s2s[n, 0] = tx
        s2s[n, 1] = tz
        cps = []
        for k in (2, 1, 3):
            cps.append(remote(
                s2s.at[n, 0, (z + k) % 4], s2r.at[n, 0, k - 1],
                s2_ss.at[n, 0, k - 1], s2_rs.at[n, 0, k - 1], at_z(k),
            ))
            cps.append(remote(
                s2s.at[n, 1, (x + k) % 4], s2r.at[n, 1, k - 1],
                s2_ss.at[n, 1, k - 1], s2_rs.at[n, 1, k - 1], at_x(k),
            ))
        s2_cp[n] = start(cps)

    def unit_e(n):
        ch, l = UNITS[n]
        cols = slice(ch * CW, (ch + 1) * CW)
        wait(s2_cp[n])
        t0 = s2s[n, 0, z]
        t1 = s2s[n, 1, x]
        for k in range(3):
            t0 = t0 + s2r[n, 0, k]
            t1 = t1 + s2r[n, 1, k]
        cg_out[l, 0:32, cols] = -t0
        cg_out[l, 32:64, cols] = -t1

    def step(t):
        for lag, op in enumerate((unit_a, unit_b, unit_c, unit_d, unit_e)):
            if 0 <= t - lag < len(UNITS):
                op(t - lag)

    H = D // 2

    def gather(turn, ss, rs):
        cps = []
        for k in (2, 1, 3):
            if turn == 1:
                va = enc_out.at[c, z, x, :, 0:H]
                vb = enc_out.at[c, z, x, :, H:D]
                da, db = at_x(k), at_z(k)
            else:
                va = enc_out.at[c, z, :, :, 0:H]
                vb = enc_out.at[c, :, x, :, H:D]
                da, db = at_z(k), at_x(k)
            cps.append(remote(va, va, ss.at[0, k - 1], rs.at[0, k - 1], da))
            cps.append(remote(vb, vb, ss.at[1, k - 1], rs.at[1, k - 1], db))
        return start(cps)

    chain(0)
    rcs_cp.wait()
    for l in range(LEVELS):
        for h, src in enumerate((rc, rcs)):
            slot_code = jnp.concatenate(
                [src[k, l : l + 1, :] for k in range(4)], axis=1
            ).astype(I32)
            rows = iota((1024, SLOTS), 0)
            code = ((rows >> 6) << 7) + c * 64 + (rows & 63) + 1
            oh[l, :, h * SLOTS : (h + 1) * SLOTS] = onehot(code == slot_code)
    enc_b(0)
    wait(f_cp[1])
    start(f_cp[2])
    f_cp[1] = []
    chain(1)
    enc_c(0)
    enc_b(1)
    step(0)
    enc_d(0)
    enc_c(1)
    step(1)
    enc_d(1)
    step(2)
    chain(2)
    out_cp += start([pltpu.make_async_copy(res_out, res_hbm, out_sem.at[0])])
    step(3)
    enc_b(2)
    step(4)
    enc_c(2)
    step(5)
    enc_d(2)
    ey_cp = start([
        remote(ey.at[y], ey.at[y], ey_ss.at[k - 1], ey_rs.at[k - 1], at_y(k)) for k in (2, 1, 3)
    ])
    step(6)
    wait(ey_cp)
    enc_out[c, z, x] = (((ey[0] + ey[1]) + ey[2]) + ey[3]) * (1.0 / (TOK * 128))
    a1_cp = gather(1, a1_ss, a1_rs)
    step(7)
    wait(a1_cp)
    a2_cp = gather(2, a2_ss, a2_rs)
    step(8)
    step(9)
    wait(a2_cp)
    a3_cp = start([remote(enc_out.at[c], enc_out.at[c], a3_ss, a3_rs, sib)])
    step(10)
    wait(a3_cp)
    out_cp += start([pltpu.make_async_copy(enc_out, enc_hbm, out_sem.at[1])])
    step(11)
    step(12)
    out_cp += start([pltpu.make_async_copy(cg_out, cg_hbm, out_sem.at[2])])
    wait(out_cp)


def store(a_hbm, b_hbm, c_hbm, ao, bo, co, av, bv, cv, in_sem, out_sem):
    pieces = []
    for k in range(2):
        for q in range(2):
            part = (k, pl.ds(2 * q, 2))
            pieces.append((b_hbm.at[part], bv.at[part], bo.at[part]))
    pieces += [(a_hbm, av, ao), (c_hbm, cv, co)]
    loads = [pltpu.make_async_copy(s, v, in_sem.at[n]) for n, (s, v, o) in enumerate(pieces)]
    stores = [pltpu.make_async_copy(v, o, out_sem.at[n]) for n, (s, v, o) in enumerate(pieces)]
    for cp in loads:
        cp.start()
    for load, back in zip(loads, stores):
        load.wait()
        back.start()
    for cp in stores:
        cp.wait()


def on_device(hidden, enc_weight, codebook, codes):
    dma = pltpu.SemaphoreType.DMA
    vmem = pltpu.VMEM
    n = len(UNITS)
    scratch = [
        vmem((TOK, D), BF16),
        vmem((D, D), BF16),
        vmem((LEVELS, SHARD, D), BF16),
        vmem((8, TOK), I32),
        vmem((4, 8, CAP), F32),
        vmem((4, 8, CAP), F32),
        vmem((4, 8, CAP), F32),
        vmem((LEVELS, SLOTS, TOK), BF16),
        vmem((LEVELS, TOK, SLOTS), BF16),
        vmem((LEVELS, 1024, 1024), BF16),
        vmem((NCH, LEVELS, 3, CAP, CW), BF16),
        vmem((NCH, LEVELS, 4, CAP, CW), BF16),
        vmem((NCH, LEVELS, 3, CAP, CW), BF16),
        vmem((NCH, LEVELS, 4, CAP, CW), BF16),
        vmem((NCH, LEVELS, 4, CAP, CW), BF16),
        vmem((RING, 4, 4, 64, CW), F32),
        vmem((n, 2, 2, 2, 32, CW), BF16),
        vmem((n, 2, 2, 2, 32, CW), BF16),
        vmem((n, 2, 2, 4, 32, CW), BF16),
        vmem((n, 2, 2, 4, 32, CW), BF16),
        vmem((n, 2, 4, 32, CW), F32),
        vmem((n, 2, 3, 32, CW), F32),
        vmem((NCH, 2, 4, 4, 24, CW), F32),
        vmem((NCH, 4, 4, 24, CW), F32),
        vmem((NCH, 2, 3, 4, 24, CW // 2), F32),
        vmem((NCH, 2, 4, 24, CW // 2), F32),
        vmem((NCH, 2, 3, 24, CW // 2), F32),
        vmem((4, 24, D), F32),
        vmem((LEVELS, 64, D), F32),
        vmem((2, 4, 4, 24, D), F32),
        vmem((TOK, D), F32),
        dma((2,)), dma((LEVELS,)), dma((3,)),
        dma((3,)), dma((3,)), dma, dma,
        dma((NCH, LEVELS, 3)), dma((NCH, LEVELS, 3)), dma((NCH, LEVELS, 3)), dma((NCH, LEVELS, 3)),
        dma((NCH, LEVELS)), dma((NCH, LEVELS)),
        dma((n, 2, 2)), dma((n, 2, 2)), dma((n, 2, 2)), dma((n, 2, 2)),
        dma((n, 2, 3)), dma((n, 2, 3)),
        dma((NCH,)), dma((NCH,)),
        dma((NCH, 2, 3)), dma((NCH, 2, 3)), dma((NCH, 2, 3)), dma((NCH, 2, 3)),
        dma((3,)), dma((3,)),
        dma((2, 3)), dma((2, 3)), dma((2, 3)), dma((2, 3)),
        dma, dma,
    ]
    in_vmem = pl.BlockSpec(memory_space=pltpu.VMEM)
    in_any = pl.BlockSpec(memory_space=pl.ANY)
    shapes = (
        jax.ShapeDtypeStruct((LEVELS, 64, D), F32),
        jax.ShapeDtypeStruct((2, 4, 4, 24, D), F32),
        jax.ShapeDtypeStruct((TOK, D), F32),
    )
    outs = pl.pallas_call(
        kernel,
        out_shape=shapes,
        in_specs=[in_any, in_any, in_any, in_vmem],
        out_specs=(in_any,) * 3,
        scratch_shapes=scratch,
        compiler_params=pltpu.CompilerParams(
            collective_id=0, has_side_effects=True, vmem_limit_bytes=62 * 2**20
        ),
        cost_estimate=pl.CostEstimate(flops=13 * 10**9, bytes_accessed=16 * 10**6, transcendentals=0),
        name="quantizer_step",
    )(hidden, enc_weight, codebook, codes)
    code_grad, enc_grad, last = pl.pallas_call(
        store,
        out_shape=shapes,
        in_specs=[in_any] * 3,
        out_specs=(in_any,) * 3,
        scratch_shapes=[vmem(o.shape, F32) for o in shapes] + [dma((6,)), dma((6,))],
        name="store",
    )(*outs)
    return code_grad[:, None], enc_grad.reshape(D, D), last


def solution(mesh):
    in_specs = (P(("items", "book"), None), P(), P(None, "book", None), P(None, ("items", "book")))
    out_specs = (P(None, "book", "items", None), P(), P(("items", "book"), None))
    return jax.shard_map(
        on_device, mesh=mesh, in_specs=in_specs, out_specs=out_specs, check_vma=False
    )
```

```python
import jax
import jax.numpy as jnp
from jax import lax
from jax.experimental import pallas as pl
from jax.experimental.pallas import tpu as pltpu
from jax.sharding import PartitionSpec as P

MESH = pl.DeviceIdType.MESH
F32 = jnp.float32
BF16 = jnp.bfloat16
I32 = jnp.int32

TOK = 256
D = 768
LEVELS = 3
SHARD = 2048
CAP = 128
SLOTS = 4 * CAP
CW = 256
NCH = D // CW
UNITS = [(ch, l) for ch in range(NCH) for l in (2, 1, 0)]
RING = 6


def onehot(mask):
    return jnp.where(mask, 1.0, 0.0).astype(BF16)


def dot(a, b):
    return jnp.dot(a, b, preferred_element_type=F32)


def iota(shape, axis):
    return lax.broadcasted_iota(I32, shape, axis)


def kernel(
    hid_hbm, w_hbm, cb_hbm, codes, cg_hbm, enc_hbm, res_hbm,
    hid, w, cb, code8, pk, rc, rcs, ut, u, oh, fs, rr, gs, gr, gsib, dd,
    fars, farr, nears, nearr, s2s, s2r, e, ec, e1r, e2s, e2r, ey, cg_out, enc_out, res_out,
    in_sem, cb_sem, out_sem, pk_ss, pk_rs, rcs_ss, rcs_rs, f_ss, f_rs, g_ss, g_rs, sib_ss, sib_rs,
    far_ss, far_rs, near_ss, near_rs, s2_ss, s2_rs, ec_ss, ec_rs, e1_ss, e1_rs, e2_ss, e2_rs,
    ey_ss, ey_rs, a1_ss, a1_rs, a2_ss, a2_rs, a3_ss, a3_rs,
):
    i = lax.axis_index("items")
    y = lax.axis_index("book")
    c = i % 2
    x = (i // 2) % 4
    z = i // 8

    def at_y(k):
        return (i, (y + k) % 4)

    def at_x(k):
        return (z * 8 + ((x + k) % 4) * 2 + c, y)

    def at_z(k):
        return (((z + k) % 4) * 8 + x * 2 + c, y)

    sib = (z * 8 + x * 2 + (1 - c), y)

    def remote(src, dst, ss, rs, dev):
        return pltpu.make_async_remote_copy(
            src_ref=src, dst_ref=dst, send_sem=ss, recv_sem=rs, device_id=dev, device_id_type=MESH
        )

    def start(cps):
        for cp in cps:
            cp.start()
        return cps

    def wait(cps):
        for cp in cps:
            cp.wait()

    def took(ref, sem):
        pltpu.make_async_copy(ref, ref, sem).wait()

    bar = pltpu.get_barrier_semaphore()
    for k in (1, 2, 3):
        pl.semaphore_signal(bar, inc=1, device_id=at_y(k), device_id_type=MESH)
        pl.semaphore_signal(bar, inc=1, device_id=at_x(k), device_id_type=MESH)
        pl.semaphore_signal(bar, inc=1, device_id=at_z(k), device_id_type=MESH)
    pl.semaphore_signal(bar, inc=1, device_id=sib, device_id_type=MESH)
    cb_cp = start([
        pltpu.make_async_copy(cb_hbm.at[l], cb.at[l], cb_sem.at[l]) for l in range(LEVELS)
    ])
    in_cp = start([
        pltpu.make_async_copy(hid_hbm, hid, in_sem.at[0]),
        pltpu.make_async_copy(w_hbm, w, in_sem.at[1]),
    ])

    code8[...] = jnp.zeros_like(code8)
    code8[0:LEVELS, :] = codes[...]
    cv = code8[...]
    dist = ((cv >> 11) - y) & 3
    val = (cv & (SHARD - 1)) + 1
    tri = onehot(iota((TOK, TOK), 0) < iota((TOK, TOK), 1))
    pos = jnp.zeros((8, TOK), F32)
    for k in range(4):
        m = jnp.where(dist == k, 1.0, 0.0)
        pos = pos + m * (k * CAP + dot(m.astype(BF16), tri))
    pos_i = pos.astype(I32)
    pos_t = pos.T.astype(I32)
    hl = jnp.concatenate([(val >> 6).astype(F32), (val & 63).astype(F32)], axis=0).astype(BF16)
    pk[...] = jnp.zeros_like(pk)
    for l in range(LEVELS):
        ul = onehot(iota((TOK, SLOTS), 1) == pos_t[:, l : l + 1])
        u[l] = ul
        pc = dot(hl, ul)
        row = pc[l : l + 1, :] * 64.0 + pc[8 + l : 9 + l, :]
        for k in range(4):
            pk[k, l : l + 1, :] = row[:, k * CAP : (k + 1) * CAP]
    rc[0] = pk[0]

    pl.semaphore_wait(bar, 10)
    start([
        remote(pk.at[k], rc.at[4 - k], pk_ss, pk_rs, at_y(k)) for k in (2, 1, 3)
    ])
    for l in range(LEVELS):
        ut[l] = onehot(iota((SLOTS, TOK), 0) == pos_i[l : l + 1, :])
    took(rc.at[1:4], pk_rs)
    remote(rc, rcs, rcs_ss, rcs_rs, sib).start()

    held = jnp.concatenate([rc[k] for k in range(4)], axis=1)
    held_t = held.T.astype(I32)

    def fetch_copies(ch, l):
        return [
            remote(
                fs.at[ch, l, k - 1], rr.at[ch, l, 4 - k],
                f_ss, f_rs.at[ch], at_y(k),
            )
            for k in (2, 1, 3)
        ]

    def fetch(ch, l):
        cols = slice(ch * CW, (ch + 1) * CW)
        got = dot(oh[l, 0:SLOTS, :], cb[l, 0:1024, cols])
        got = got + dot(oh[l, SLOTS:, :], cb[l, 1024:2048, cols])
        got = got.astype(BF16)
        rr[ch, l, 0] = got[0:CAP]
        for k in (1, 2, 3):
            fs[ch, l, k - 1] = got[k * CAP : (k + 1) * CAP]

    for l in range(LEVELS):
        col = held_t[:, l : l + 1]
        for h in range(2):
            oh[l, h * SLOTS : (h + 1) * SLOTS, :] = onehot(
                iota((SLOTS, 1024), 1) + (1 + h * 1024) == col
            )
        cb_cp[l].wait()
        fetch(0, l)
        start(fetch_copies(0, l))
    for ch in (1, 2):
        for l in range(LEVELS):
            fetch(ch, l)
            if ch == 1:
                start(fetch_copies(1, l))
    wait(in_cp)

    def chain(ch):
        cols = slice(ch * CW, (ch + 1) * CW)
        took(rr.at[ch, :, 1:4], f_rs.at[ch])
        r = dot(hid[...], w[:, cols])
        res = []
        for l in range(LEVELS):
            r = r - dot(u[l], rr[ch, l].reshape(SLOTS, CW))
            res.append(r)
        carried = jnp.zeros_like(r)
        for l in reversed(range(LEVELS)):
            carried = carried + res[l]
            cl = carried.astype(BF16)
            packed = dot(ut[l], cl).astype(BF16)
            gr[ch, l, 0] = packed[0:CAP]
            for k in (1, 2, 3):
                gs[ch, l, k - 1] = packed[k * CAP : (k + 1) * CAP]
            start([
                remote(
                    gs.at[ch, l, k - 1], gr.at[ch, l, 4 - k],
                    g_ss, g_rs.at[ch, l], at_y(k),
                )
                for k in (2, 1, 3)
            ])
        res_out[:, cols] = r
        prod = lax.dot_general(
            hid[...], cl, (((0,), (0,)), ((), ())), preferred_element_type=F32
        )
        e[ch] = prod.reshape(2, 4, 4, 24, CW)
        remote(e.at[ch, 1 - c], ec.at[ch], ec_ss, ec_rs.at[ch], sib).start()

    out_cp = []

    HW = CW // 2

    def enc_b(ch):
        took(ec.at[ch], ec_rs.at[ch])
        e[ch, c] = e[ch, c] + ec[ch]
        cps = []
        for k in (2, 1, 3):
            cps.append(remote(
                e.at[ch, c, :, (x + k) % 4, :, 0:HW], e1r.at[ch, 0, k - 1],
                e1_ss, e1_rs.at[ch], at_x(k),
            ))
            cps.append(remote(
                e.at[ch, c, (z + k) % 4, :, :, HW:CW], e1r.at[ch, 1, k - 1],
                e1_ss, e1_rs.at[ch], at_z(k),
            ))
        start(cps)

    def enc_c(ch):
        took(e1r.at[ch], e1_rs.at[ch])
        t0 = e[ch, c, :, x, :, 0:HW]
        t1 = e[ch, c, z, :, :, HW:CW]
        for k in range(3):
            t0 = t0 + e1r[ch, 0, k]
            t1 = t1 + e1r[ch, 1, k]
        e2s[ch, 0] = t0
        e2s[ch, 1] = t1
        cps = []
        for k in (2, 1, 3):
            cps.append(remote(
                e2s.at[ch, 0, (z + k) % 4], e2r.at[ch, 0, k - 1],
                e2_ss, e2_rs.at[ch], at_z(k),
            ))
            cps.append(remote(
                e2s.at[ch, 1, (x + k) % 4], e2r.at[ch, 1, k - 1],
                e2_ss, e2_rs.at[ch], at_x(k),
            ))
        start(cps)

    def enc_d(ch):
        took(e2r.at[ch], e2_rs.at[ch])
        t0 = e2s[ch, 0, z]
        t1 = e2s[ch, 1, x]
        for k in range(3):
            t0 = t0 + e2r[ch, 0, k]
            t1 = t1 + e2r[ch, 1, k]
        ey[ch, y, :, 0:HW] = t0
        ey[ch, y, :, HW:CW] = t1
        start([
            remote(ey.at[ch, y], ey.at[ch, y], ey_ss, ey_rs.at[ch], at_y(k)) for k in (2, 1, 3)
        ])

    def gather(ch, turn, ss, rs):
        lo = slice(ch * CW, ch * CW + HW)
        hi = slice(ch * CW + HW, (ch + 1) * CW)
        cps = []
        for k in (2, 1, 3):
            if turn == 1:
                va = enc_out.at[c, z, x, :, lo]
                vb = enc_out.at[c, z, x, :, hi]
                da, db = at_x(k), at_z(k)
            else:
                va = enc_out.at[c, z, :, :, lo]
                vb = enc_out.at[c, :, x, :, hi]
                da, db = at_z(k), at_x(k)
            cps.append(remote(va, va, ss, rs.at[ch], da))
            cps.append(remote(vb, vb, ss, rs.at[ch], db))
        start(cps)

    def enc_e(ch):
        took(ey.at[ch, 0:3], ey_rs.at[ch])
        total = ((ey[ch, 0] + ey[ch, 1]) + ey[ch, 2]) + ey[ch, 3]
        enc_out[c, z, x, :, ch * CW : (ch + 1) * CW] = total * (1.0 / (TOK * 128))
        gather(ch, 1, a1_ss, a1_rs)

    def enc_f(ch):
        took(ey.at[ch, 0:3], a1_rs.at[ch])
        gather(ch, 2, a2_ss, a2_rs)

    def enc_g(ch):
        took(ec.at[ch, 0:3], a2_rs.at[ch])
        part = enc_out.at[c, :, :, :, ch * CW : (ch + 1) * CW]
        remote(part, part, a3_ss, a3_rs.at[ch], sib).start()

    def enc_h(ch):
        cols = slice(ch * CW, (ch + 1) * CW)
        took(enc_out.at[1 - c, :, :, :, cols], a3_rs.at[ch])
        out_cp.extend(start([pltpu.make_async_copy(
            enc_out.at[:, :, :, :, cols], enc_hbm.at[:, :, :, :, cols], out_sem.at[1 + ch]
        )]))


    def unit_a(n):
        ch, l = UNITS[n]
        took(gr.at[ch, l, 1:4], g_rs.at[ch, l])
        remote(gr.at[ch, l], gsib.at[ch, l], sib_ss, sib_rs.at[ch, l], sib).start()

    def unit_b(n):
        ch, l = UNITS[n]
        q = n % RING
        acc = dot(oh[l, :, 0:SLOTS], gr[ch, l].reshape(SLOTS, CW))
        took(gsib.at[ch, l], sib_rs.at[ch, l])
        acc = acc + dot(oh[l, :, SLOTS:], gsib[ch, l].reshape(SLOTS, CW))
        dd[q] = acc.reshape(4, 4, 64, CW)
        x2 = (x + 2) % 4
        z2 = (z + 2) % 4
        cps = []
        for d, k in enumerate((1, 3)):
            fars[n, 0, d] = dd[q, 2 * d : 2 * d + 2, x2, 0:32, :].astype(BF16)
            fars[n, 1, d] = dd[q, z2, 2 * d : 2 * d + 2, 32:64, :].astype(BF16)
            for h, at in enumerate((at_x, at_z)):
                cps.append(remote(
                    fars.at[n, h, d], farr.at[n, h, d],
                    far_ss, far_rs.at[n], at(k),
                ))
        start(cps)

    def unit_c(n):
        q = n % RING
        took(farr.at[n], far_rs.at[n])
        cps = []
        for d, k in enumerate((1, 3)):
            xk = (x + k) % 4
            zk = (z + k) % 4
            a, b = 2 * d, 2 - 2 * d
            nears[n, 0, d, a : a + 2] = (
                dd[q, a : a + 2, xk, 0:32, :] + farr[n, 0, d].astype(F32)
            ).astype(BF16)
            nears[n, 0, d, b : b + 2] = dd[q, b : b + 2, xk, 0:32, :].astype(BF16)
            nears[n, 1, d, a : a + 2] = (
                dd[q, zk, a : a + 2, 32:64, :] + farr[n, 1, d].astype(F32)
            ).astype(BF16)
            nears[n, 1, d, b : b + 2] = dd[q, zk, b : b + 2, 32:64, :].astype(BF16)
            for h, at in enumerate((at_x, at_z)):
                cps.append(remote(
                    nears.at[n, h, d], nearr.at[n, h, d],
                    near_ss, near_rs.at[n], at(k),
                ))
        start(cps)

    def unit_d(n):
        q = n % RING
        took(nearr.at[n], near_rs.at[n])
        tx = dd[q, :, x, 0:32, :]
        tz = dd[q, z, :, 32:64, :]
        for d in range(2):
            tx = tx + nearr[n, 0, d].astype(F32)
            tz = tz + nearr[n, 1, d].astype(F32)
        s2s[n, 0] = tx
        s2s[n, 1] = tz
        cps = []
        for k in (2, 1, 3):
            cps.append(remote(
                s2s.at[n, 0, (z + k) % 4], s2r.at[n, 0, k - 1],
                s2_ss, s2_rs.at[n], at_z(k),
            ))
            cps.append(remote(
                s2s.at[n, 1, (x + k) % 4], s2r.at[n, 1, k - 1],
                s2_ss, s2_rs.at[n], at_x(k),
            ))
        start(cps)

    def unit_e(n):
        ch, l = UNITS[n]
        cols = slice(ch * CW, (ch + 1) * CW)
        took(s2r.at[n], s2_rs.at[n])
        t0 = s2s[n, 0, z]
        t1 = s2s[n, 1, x]
        for k in range(3):
            t0 = t0 + s2r[n, 0, k]
            t1 = t1 + s2r[n, 1, k]
        cg_out[l, 0:32, cols] = -t0
        cg_out[l, 32:64, cols] = -t1

    def code_store(ch):
        cols = slice(ch * CW, (ch + 1) * CW)
        out_cp.extend(start([pltpu.make_async_copy(
            cg_out.at[:, :, cols], cg_hbm.at[:, :, cols], out_sem.at[4 + ch]
        )]))

    def own_codes():
        took(rcs, rcs_rs)
        for l in range(LEVELS):
            for h, src in enumerate((rc, rcs)):
                slot_code = jnp.concatenate(
                    [src[k, l : l + 1, :] for k in range(4)], axis=1
                ).astype(I32)
                rows = iota((1024, SLOTS), 0)
                code = ((rows >> 6) << 7) + c * 64 + (rows & 63) + 1
                oh[l, :, h * SLOTS : (h + 1) * SLOTS] = onehot(code == slot_code)

    own_codes()
    chain(0)
    enc_b(0)
    enc_c(0)
    chain(1)
    for l in range(LEVELS):
        start(fetch_copies(2, l))
    enc_d(0)
    unit_a(0)
    enc_b(1)
    unit_b(0)
    unit_a(1)
    unit_b(1)
    unit_c(0)
    enc_c(1)
    unit_a(2)
    unit_b(2)
    unit_c(1)
    unit_a(3)
    unit_d(0)
    unit_b(3)
    unit_a(4)
    enc_d(1)
    unit_c(2)
    unit_d(1)
    unit_b(4)
    unit_c(3)
    unit_a(5)
    unit_e(0)
    unit_b(5)
    unit_e(1)
    unit_c(4)
    unit_d(2)
    unit_c(5)
    unit_d(3)
    unit_d(4)
    chain(2)
    out_cp += start([pltpu.make_async_copy(res_out, res_hbm, out_sem.at[0])])
    enc_e(0)
    unit_e(2)
    code_store(0)
    unit_d(5)
    enc_b(2)
    enc_e(1)
    unit_e(3)
    enc_f(0)
    unit_e(4)
    unit_a(6)
    unit_e(5)
    code_store(1)
    unit_b(6)
    enc_c(2)
    unit_a(7)
    enc_f(1)
    unit_b(7)
    unit_a(8)
    unit_c(6)
    enc_d(2)
    unit_b(8)
    enc_g(1)
    unit_c(7)
    enc_e(2)
    unit_d(6)
    unit_c(8)
    enc_h(1)
    enc_g(0)
    enc_h(0)
    enc_f(2)
    unit_d(7)
    unit_e(6)
    unit_d(8)
    enc_g(2)
    unit_e(7)
    enc_h(2)
    unit_e(8)
    code_store(2)
    for ref, sem in (
        (pk.at[1:4], pk_ss), (rc, rcs_ss), (fs, f_ss), (gs, g_ss), (gr, sib_ss), (fars, far_ss),
        (nears, near_ss), (s2r, s2_ss), (ec, ec_ss), (e1r, e1_ss), (e2r, e2_ss), (ey.at[:, 0:3], ey_ss),
        (ey.at[:, 0:3], a1_ss), (ec.at[:, 0:3], a2_ss), (ec, a3_ss),
    ):
        took(ref, sem)
    wait(out_cp)


def store(a_hbm, b_hbm, c_hbm, ao, bo, co, av, bv, cv, in_sem, out_sem):
    pieces = []
    for k in range(2):
        for q in range(2):
            part = (k, pl.ds(2 * q, 2))
            pieces.append((b_hbm.at[part], bv.at[part], bo.at[part]))
    pieces += [(a_hbm, av, ao), (c_hbm, cv, co)]
    loads = [pltpu.make_async_copy(s, v, in_sem.at[n]) for n, (s, v, o) in enumerate(pieces)]
    stores = [pltpu.make_async_copy(v, o, out_sem.at[n]) for n, (s, v, o) in enumerate(pieces)]
    for cp in loads:
        cp.start()
    for load, back in zip(loads, stores):
        load.wait()
        back.start()
    for cp in stores:
        cp.wait()


def on_device(hidden, enc_weight, codebook, codes):
    dma = pltpu.SemaphoreType.DMA
    vmem = pltpu.VMEM
    n = len(UNITS)
    scratch = [
        vmem((TOK, D), BF16),
        vmem((D, D), BF16),
        vmem((LEVELS, SHARD, D), BF16),
        vmem((8, TOK), I32),
        vmem((4, 8, CAP), F32),
        vmem((4, 8, CAP), F32),
        vmem((4, 8, CAP), F32),
        vmem((LEVELS, SLOTS, TOK), BF16),
        vmem((LEVELS, TOK, SLOTS), BF16),
        vmem((LEVELS, 1024, 1024), BF16),
        vmem((NCH, LEVELS, 3, CAP, CW), BF16),
        vmem((NCH, LEVELS, 4, CAP, CW), BF16),
        vmem((NCH, LEVELS, 3, CAP, CW), BF16),
        vmem((NCH, LEVELS, 4, CAP, CW), BF16),
        vmem((NCH, LEVELS, 4, CAP, CW), BF16),
        vmem((RING, 4, 4, 64, CW), F32),
        vmem((n, 2, 2, 2, 32, CW), BF16),
        vmem((n, 2, 2, 2, 32, CW), BF16),
        vmem((n, 2, 2, 4, 32, CW), BF16),
        vmem((n, 2, 2, 4, 32, CW), BF16),
        vmem((n, 2, 4, 32, CW), F32),
        vmem((n, 2, 3, 32, CW), F32),
        vmem((NCH, 2, 4, 4, 24, CW), F32),
        vmem((NCH, 4, 4, 24, CW), F32),
        vmem((NCH, 2, 3, 4, 24, CW // 2), F32),
        vmem((NCH, 2, 4, 24, CW // 2), F32),
        vmem((NCH, 2, 3, 24, CW // 2), F32),
        vmem((NCH, 4, 24, CW), F32),
        vmem((LEVELS, 64, D), F32),
        vmem((2, 4, 4, 24, D), F32),
        vmem((TOK, D), F32),
        dma((2,)), dma((LEVELS,)), dma((1 + 2 * NCH,)),
        dma, dma, dma, dma,
        dma, dma((NCH,)), dma, dma((NCH, LEVELS)), dma, dma((NCH, LEVELS)),
        dma, dma((n,)), dma, dma((n,)), dma, dma((n,)),
        dma, dma((NCH,)), dma, dma((NCH,)), dma, dma((NCH,)),
        dma, dma((NCH,)), dma, dma((NCH,)), dma, dma((NCH,)), dma, dma((NCH,)),
    ]
    in_vmem = pl.BlockSpec(memory_space=pltpu.VMEM)
    in_any = pl.BlockSpec(memory_space=pl.ANY)
    shapes = (
        jax.ShapeDtypeStruct((LEVELS, 64, D), F32),
        jax.ShapeDtypeStruct((2, 4, 4, 24, D), F32),
        jax.ShapeDtypeStruct((TOK, D), F32),
    )
    outs = pl.pallas_call(
        kernel,
        out_shape=shapes,
        in_specs=[in_any, in_any, in_any, in_vmem],
        out_specs=(in_any,) * 3,
        scratch_shapes=scratch,
        compiler_params=pltpu.CompilerParams(
            collective_id=0, has_side_effects=True, vmem_limit_bytes=62 * 2**20
        ),
        cost_estimate=pl.CostEstimate(flops=13 * 10**9, bytes_accessed=16 * 10**6, transcendentals=0),
        name="quantizer_step",
    )(hidden, enc_weight, codebook, codes)
    code_grad, enc_grad, last = pl.pallas_call(
        store,
        out_shape=shapes,
        in_specs=[in_any] * 3,
        out_specs=(in_any,) * 3,
        scratch_shapes=[vmem(o.shape, F32) for o in shapes] + [dma((6,)), dma((6,))],
        name="store",
    )(*outs)
    return code_grad[:, None], enc_grad.reshape(D, D), last


def solution(mesh):
    in_specs = (P(("items", "book"), None), P(), P(None, "book", None), P(None, ("items", "book")))
    out_specs = (P(None, "book", "items", None), P(), P(("items", "book"), None))
    return jax.shard_map(
        on_device, mesh=mesh, in_specs=in_specs, out_specs=out_specs, check_vma=False
    )
```

```python
import jax
import jax.numpy as jnp
from jax import lax
from jax.experimental import pallas as pl
from jax.experimental.pallas import tpu as pltpu
from jax.sharding import PartitionSpec as P

MESH = pl.DeviceIdType.MESH
F32 = jnp.float32
BF16 = jnp.bfloat16
I32 = jnp.int32

TOK = 256
D = 768
LEVELS = 3
SHARD = 2048
CAP = 128
SLOTS = 4 * CAP
CW = 256
NCH = D // CW
UNITS = [(ch, l) for ch in range(NCH) for l in (2, 1, 0)]
RING = 6


def onehot(mask):
    return jnp.where(mask, 1.0, 0.0).astype(BF16)


def dot(a, b):
    return jnp.dot(a, b, preferred_element_type=F32)


def iota(shape, axis):
    return lax.broadcasted_iota(I32, shape, axis)


def kernel(
    hid_hbm, w_hbm, cb_hbm, codes, cg_out, enc_out, res_out,
    hid, w, cb, code8, pk, rc, rcs, ut, u, oh, fs, rr, gs, gr, gsib, dd,
    fars, farr, nears, nearr, s2s, s2r, e, ec, e1r, e2s, e2r, ey,
    in_sem, cb_sem, pk_ss, pk_rs, rcs_ss, rcs_rs, f_ss, f_rs, g_ss, g_rs, sib_ss, sib_rs,
    far_ss, far_rs, near_ss, near_rs, s2_ss, s2_rs, ec_ss, ec_rs, e1_ss, e1_rs, e2_ss, e2_rs,
    ey_ss, ey_rs, a1_ss, a1_rs, a2_ss, a2_rs, a3_ss, a3_rs,
):
    i = lax.axis_index("items")
    y = lax.axis_index("book")
    c = i % 2
    x = (i // 2) % 4
    z = i // 8

    def at_y(k):
        return (i, (y + k) % 4)

    def at_x(k):
        return (z * 8 + ((x + k) % 4) * 2 + c, y)

    def at_z(k):
        return (((z + k) % 4) * 8 + x * 2 + c, y)

    sib = (z * 8 + x * 2 + (1 - c), y)

    def remote(src, dst, ss, rs, dev):
        return pltpu.make_async_remote_copy(
            src_ref=src, dst_ref=dst, send_sem=ss, recv_sem=rs, device_id=dev, device_id_type=MESH
        )

    def start(cps):
        for cp in cps:
            cp.start()
        return cps

    def wait(cps):
        for cp in cps:
            cp.wait()

    def took(ref, sem):
        pltpu.make_async_copy(ref, ref, sem).wait()

    bar = pltpu.get_barrier_semaphore()
    for k in (1, 2, 3):
        pl.semaphore_signal(bar, inc=1, device_id=at_y(k), device_id_type=MESH)
        pl.semaphore_signal(bar, inc=1, device_id=at_x(k), device_id_type=MESH)
        pl.semaphore_signal(bar, inc=1, device_id=at_z(k), device_id_type=MESH)
    pl.semaphore_signal(bar, inc=1, device_id=sib, device_id_type=MESH)
    cb_cp = start([
        pltpu.make_async_copy(cb_hbm.at[l], cb.at[l], cb_sem.at[l]) for l in range(LEVELS)
    ])
    in_cp = start([
        pltpu.make_async_copy(hid_hbm, hid, in_sem.at[0]),
        pltpu.make_async_copy(w_hbm, w, in_sem.at[1]),
    ])

    code8[...] = jnp.zeros_like(code8)
    code8[0:LEVELS, :] = codes[...]
    cv = code8[...]
    dist = ((cv >> 11) - y) & 3
    val = (cv & (SHARD - 1)) + 1
    tri = onehot(iota((TOK, TOK), 0) < iota((TOK, TOK), 1))
    pos = jnp.zeros((8, TOK), F32)
    for k in range(4):
        m = jnp.where(dist == k, 1.0, 0.0)
        pos = pos + m * (k * CAP + dot(m.astype(BF16), tri))
    pos_i = pos.astype(I32)
    pos_t = pos.T.astype(I32)
    hl = jnp.concatenate([(val >> 6).astype(F32), (val & 63).astype(F32)], axis=0).astype(BF16)
    pk[...] = jnp.zeros_like(pk)
    for l in range(LEVELS):
        ul = onehot(iota((TOK, SLOTS), 1) == pos_t[:, l : l + 1])
        u[l] = ul
        pc = dot(hl, ul)
        row = pc[l : l + 1, :] * 64.0 + pc[8 + l : 9 + l, :]
        for k in range(4):
            pk[k, l : l + 1, :] = row[:, k * CAP : (k + 1) * CAP]
    rc[0] = pk[0]

    pl.semaphore_wait(bar, 10)
    start([
        remote(pk.at[k], rc.at[4 - k], pk_ss, pk_rs, at_y(k)) for k in (2, 1, 3)
    ])
    for l in range(LEVELS):
        ut[l] = onehot(iota((SLOTS, TOK), 0) == pos_i[l : l + 1, :])
    took(rc.at[1:4], pk_rs)
    remote(rc, rcs, rcs_ss, rcs_rs, sib).start()

    held = jnp.concatenate([rc[k] for k in range(4)], axis=1)
    held_t = held.T.astype(I32)

    def fetch_copies(ch, l):
        return [
            remote(
                fs.at[ch, l, k - 1], rr.at[ch, l, 4 - k],
                f_ss, f_rs.at[ch], at_y(k),
            )
            for k in (2, 1, 3)
        ]

    def fetch(ch, l):
        cols = slice(ch * CW, (ch + 1) * CW)
        got = dot(oh[l, 0:SLOTS, :], cb[l, 0:1024, cols])
        got = got + dot(oh[l, SLOTS:, :], cb[l, 1024:2048, cols])
        got = got.astype(BF16)
        rr[ch, l, 0] = got[0:CAP]
        for k in (1, 2, 3):
            fs[ch, l, k - 1] = got[k * CAP : (k + 1) * CAP]

    for l in range(LEVELS):
        col = held_t[:, l : l + 1]
        for h in range(2):
            oh[l, h * SLOTS : (h + 1) * SLOTS, :] = onehot(
                iota((SLOTS, 1024), 1) + (1 + h * 1024) == col
            )
        cb_cp[l].wait()
        fetch(0, l)
        start(fetch_copies(0, l))
    for ch in (1, 2):
        for l in range(LEVELS):
            fetch(ch, l)
            if ch == 1:
                start(fetch_copies(1, l))
    wait(in_cp)

    def chain(ch):
        cols = slice(ch * CW, (ch + 1) * CW)
        took(rr.at[ch, :, 1:4], f_rs.at[ch])
        r = dot(hid[...], w[:, cols])
        res = []
        for l in range(LEVELS):
            r = r - dot(u[l], rr[ch, l].reshape(SLOTS, CW))
            res.append(r)
        carried = jnp.zeros_like(r)
        for l in reversed(range(LEVELS)):
            carried = carried + res[l]
            cl = carried.astype(BF16)
            packed = dot(ut[l], cl).astype(BF16)
            gr[ch, l, 0] = packed[0:CAP]
            for k in (1, 2, 3):
                gs[ch, l, k - 1] = packed[k * CAP : (k + 1) * CAP]
            start([
                remote(
                    gs.at[ch, l, k - 1], gr.at[ch, l, 4 - k],
                    g_ss, g_rs.at[ch, l], at_y(k),
                )
                for k in (2, 1, 3)
            ])
            if (ch, l) == (1, 1):
                for fl in range(LEVELS):
                    start(fetch_copies(2, fl))
        res_out[:, cols] = r
        prod = lax.dot_general(
            hid[...], cl, (((0,), (0,)), ((), ())), preferred_element_type=F32
        )
        e[ch] = prod.reshape(2, 4, 4, 24, CW)
        remote(e.at[ch, 1 - c], ec.at[ch], ec_ss, ec_rs.at[ch], sib).start()

    HW = CW // 2

    def enc_b(ch):
        took(ec.at[ch], ec_rs.at[ch])
        e[ch, c] = e[ch, c] + ec[ch]
        cps = []
        for k in (2, 1, 3):
            cps.append(remote(
                e.at[ch, c, :, (x + k) % 4, :, 0:HW], e1r.at[ch, 0, k - 1],
                e1_ss, e1_rs.at[ch], at_x(k),
            ))
            cps.append(remote(
                e.at[ch, c, (z + k) % 4, :, :, HW:CW], e1r.at[ch, 1, k - 1],
                e1_ss, e1_rs.at[ch], at_z(k),
            ))
        start(cps)

    def enc_c(ch):
        took(e1r.at[ch], e1_rs.at[ch])
        t0 = e[ch, c, :, x, :, 0:HW]
        t1 = e[ch, c, z, :, :, HW:CW]
        for k in range(3):
            t0 = t0 + e1r[ch, 0, k]
            t1 = t1 + e1r[ch, 1, k]
        e2s[ch, 0] = t0
        e2s[ch, 1] = t1
        cps = []
        for k in (2, 1, 3):
            cps.append(remote(
                e2s.at[ch, 0, (z + k) % 4], e2r.at[ch, 0, k - 1],
                e2_ss, e2_rs.at[ch], at_z(k),
            ))
            cps.append(remote(
                e2s.at[ch, 1, (x + k) % 4], e2r.at[ch, 1, k - 1],
                e2_ss, e2_rs.at[ch], at_x(k),
            ))
        start(cps)

    def enc_d(ch):
        took(e2r.at[ch], e2_rs.at[ch])
        t0 = e2s[ch, 0, z]
        t1 = e2s[ch, 1, x]
        for k in range(3):
            t0 = t0 + e2r[ch, 0, k]
            t1 = t1 + e2r[ch, 1, k]
        ey[ch, y, :, 0:HW] = t0
        ey[ch, y, :, HW:CW] = t1
        start([
            remote(ey.at[ch, y], ey.at[ch, y], ey_ss, ey_rs.at[ch], at_y(k)) for k in (2, 1, 3)
        ])

    def gather(ch, turn, ss, rs):
        lo = slice(ch * CW, ch * CW + HW)
        hi = slice(ch * CW + HW, (ch + 1) * CW)
        cps = []
        for k in (2, 1, 3):
            if turn == 1:
                va = enc_out.at[c, z, x, :, lo]
                vb = enc_out.at[c, z, x, :, hi]
                da, db = at_x(k), at_z(k)
            else:
                va = enc_out.at[c, z, :, :, lo]
                vb = enc_out.at[c, :, x, :, hi]
                da, db = at_z(k), at_x(k)
            cps.append(remote(va, va, ss, rs.at[ch], da))
            cps.append(remote(vb, vb, ss, rs.at[ch], db))
        start(cps)

    def enc_e(ch):
        took(ey.at[ch, 0:3], ey_rs.at[ch])
        total = ((ey[ch, 0] + ey[ch, 1]) + ey[ch, 2]) + ey[ch, 3]
        enc_out[c, z, x, :, ch * CW : (ch + 1) * CW] = total * (1.0 / (TOK * 128))
        gather(ch, 1, a1_ss, a1_rs)

    def enc_f(ch):
        took(ey.at[ch, 0:3], a1_rs.at[ch])
        gather(ch, 2, a2_ss, a2_rs)

    def enc_g(ch):
        took(ec.at[ch, 0:3], a2_rs.at[ch])
        part = enc_out.at[c, :, :, :, ch * CW : (ch + 1) * CW]
        remote(part, part, a3_ss, a3_rs.at[ch], sib).start()

    def enc_h(ch):
        cols = slice(ch * CW, (ch + 1) * CW)
        took(enc_out.at[1 - c, :, :, :, cols], a3_rs.at[ch])


    def unit_a(n):
        ch, l = UNITS[n]
        took(gr.at[ch, l, 1:4], g_rs.at[ch, l])
        remote(gr.at[ch, l], gsib.at[ch, l], sib_ss, sib_rs.at[ch, l], sib).start()

    def unit_b(n):
        ch, l = UNITS[n]
        q = n % RING
        acc = dot(oh[l, :, 0:SLOTS], gr[ch, l].reshape(SLOTS, CW))
        took(gsib.at[ch, l], sib_rs.at[ch, l])
        acc = acc + dot(oh[l, :, SLOTS:], gsib[ch, l].reshape(SLOTS, CW))
        dd[q] = acc.reshape(4, 4, 64, CW)
        x2 = (x + 2) % 4
        z2 = (z + 2) % 4
        cps = []
        for d, k in enumerate((1, 3)):
            fars[n, 0, d] = dd[q, 2 * d : 2 * d + 2, x2, 0:32, :].astype(BF16)
            fars[n, 1, d] = dd[q, z2, 2 * d : 2 * d + 2, 32:64, :].astype(BF16)
            for h, at in enumerate((at_x, at_z)):
                cps.append(remote(
                    fars.at[n, h, d], farr.at[n, h, d],
                    far_ss, far_rs.at[n], at(k),
                ))
        start(cps)

    def unit_c(n):
        q = n % RING
        took(farr.at[n], far_rs.at[n])
        cps = []
        for d, k in enumerate((1, 3)):
            xk = (x + k) % 4
            zk = (z + k) % 4
            a, b = 2 * d, 2 - 2 * d
            nears[n, 0, d, a : a + 2] = (
                dd[q, a : a + 2, xk, 0:32, :] + farr[n, 0, d].astype(F32)
            ).astype(BF16)
            nears[n, 0, d, b : b + 2] = dd[q, b : b + 2, xk, 0:32, :].astype(BF16)
            nears[n, 1, d, a : a + 2] = (
                dd[q, zk, a : a + 2, 32:64, :] + farr[n, 1, d].astype(F32)
            ).astype(BF16)
            nears[n, 1, d, b : b + 2] = dd[q, zk, b : b + 2, 32:64, :].astype(BF16)
            for h, at in enumerate((at_x, at_z)):
                cps.append(remote(
                    nears.at[n, h, d], nearr.at[n, h, d],
                    near_ss, near_rs.at[n], at(k),
                ))
        start(cps)

    def unit_d(n):
        q = n % RING
        took(nearr.at[n], near_rs.at[n])
        tx = dd[q, :, x, 0:32, :]
        tz = dd[q, z, :, 32:64, :]
        for d in range(2):
            tx = tx + nearr[n, 0, d].astype(F32)
            tz = tz + nearr[n, 1, d].astype(F32)
        s2s[n, 0] = tx
        s2s[n, 1] = tz
        cps = []
        for k in (2, 1, 3):
            cps.append(remote(
                s2s.at[n, 0, (z + k) % 4], s2r.at[n, 0, k - 1],
                s2_ss, s2_rs.at[n], at_z(k),
            ))
            cps.append(remote(
                s2s.at[n, 1, (x + k) % 4], s2r.at[n, 1, k - 1],
                s2_ss, s2_rs.at[n], at_x(k),
            ))
        start(cps)

    def unit_e(n):
        ch, l = UNITS[n]
        cols = slice(ch * CW, (ch + 1) * CW)
        took(s2r.at[n], s2_rs.at[n])
        t0 = s2s[n, 0, z]
        t1 = s2s[n, 1, x]
        for k in range(3):
            t0 = t0 + s2r[n, 0, k]
            t1 = t1 + s2r[n, 1, k]
        cg_out[l, 0:32, cols] = -t0
        cg_out[l, 32:64, cols] = -t1

    def own_codes():
        took(rcs, rcs_rs)
        for l in range(LEVELS):
            for h, src in enumerate((rc, rcs)):
                slot_code = jnp.concatenate(
                    [src[k, l : l + 1, :] for k in range(4)], axis=1
                ).astype(I32)
                rows = iota((1024, SLOTS), 0)
                code = ((rows >> 6) << 7) + c * 64 + (rows & 63) + 1
                oh[l, :, h * SLOTS : (h + 1) * SLOTS] = onehot(code == slot_code)

    own_codes()
    chain(0)
    enc_b(0)
    enc_c(0)
    chain(1)
    unit_a(0)
    enc_d(0)
    enc_b(1)
    unit_b(0)
    unit_a(1)
    unit_b(1)
    unit_a(2)
    enc_c(1)
    unit_b(2)
    unit_c(0)
    unit_a(3)
    unit_c(1)
    unit_b(3)
    enc_d(1)
    unit_c(2)
    unit_a(4)
    unit_d(0)
    unit_b(4)
    unit_d(1)
    unit_c(3)
    unit_d(2)
    unit_e(0)
    unit_c(4)
    chain(2)
    unit_d(3)
    unit_e(1)
    unit_a(5)
    enc_b(2)
    unit_e(2)
    enc_e(0)
    unit_d(4)
    unit_b(5)
    enc_e(1)
    unit_e(3)
    unit_a(6)
    enc_c(2)
    enc_f(0)
    unit_b(6)
    unit_e(4)
    unit_a(7)
    unit_c(5)
    enc_f(1)
    unit_b(7)
    enc_d(2)
    unit_a(8)
    enc_g(0)
    unit_c(6)
    unit_b(8)
    unit_d(5)
    enc_h(0)
    enc_e(2)
    enc_g(1)
    unit_c(7)
    unit_d(6)
    enc_h(1)
    unit_c(8)
    unit_e(5)
    enc_f(2)
    unit_d(7)
    unit_e(6)
    unit_d(8)
    enc_g(2)
    unit_e(7)
    enc_h(2)
    unit_e(8)
    for ref, sem in (
        (pk.at[1:4], pk_ss), (rc, rcs_ss), (fs, f_ss), (gs, g_ss), (gr, sib_ss), (fars, far_ss),
        (nears, near_ss), (s2r, s2_ss), (ec, ec_ss), (e1r, e1_ss), (e2r, e2_ss), (ey.at[:, 0:3], ey_ss),
        (ey.at[:, 0:3], a1_ss), (ec.at[:, 0:3], a2_ss), (ec, a3_ss),
    ):
        took(ref, sem)


def store(a, b, c, ao, bo, co, sem):
    cps = [pltpu.make_async_copy(b.at[k], bo.at[k], sem.at[k]) for k in range(2)]
    cps += [pltpu.make_async_copy(a, ao, sem.at[2]), pltpu.make_async_copy(c, co, sem.at[3])]
    for cp in cps:
        cp.start()
    for cp in cps:
        cp.wait()


def on_device(hidden, enc_weight, codebook, codes):
    dma = pltpu.SemaphoreType.DMA
    vmem = pltpu.VMEM
    n = len(UNITS)
    scratch = [
        vmem((TOK, D), BF16),
        vmem((D, D), BF16),
        vmem((LEVELS, SHARD, D), BF16),
        vmem((8, TOK), I32),
        vmem((4, 8, CAP), F32),
        vmem((4, 8, CAP), F32),
        vmem((4, 8, CAP), F32),
        vmem((LEVELS, SLOTS, TOK), BF16),
        vmem((LEVELS, TOK, SLOTS), BF16),
        vmem((LEVELS, 1024, 1024), BF16),
        vmem((NCH, LEVELS, 3, CAP, CW), BF16),
        vmem((NCH, LEVELS, 4, CAP, CW), BF16),
        vmem((NCH, LEVELS, 3, CAP, CW), BF16),
        vmem((NCH, LEVELS, 4, CAP, CW), BF16),
        vmem((NCH, LEVELS, 4, CAP, CW), BF16),
        vmem((RING, 4, 4, 64, CW), F32),
        vmem((n, 2, 2, 2, 32, CW), BF16),
        vmem((n, 2, 2, 2, 32, CW), BF16),
        vmem((n, 2, 2, 4, 32, CW), BF16),
        vmem((n, 2, 2, 4, 32, CW), BF16),
        vmem((n, 2, 4, 32, CW), F32),
        vmem((n, 2, 3, 32, CW), F32),
        vmem((NCH, 2, 4, 4, 24, CW), F32),
        vmem((NCH, 4, 4, 24, CW), F32),
        vmem((NCH, 2, 3, 4, 24, CW // 2), F32),
        vmem((NCH, 2, 4, 24, CW // 2), F32),
        vmem((NCH, 2, 3, 24, CW // 2), F32),
        vmem((NCH, 4, 24, CW), F32),
        dma((2,)), dma((LEVELS,)),
        dma, dma, dma, dma,
        dma, dma((NCH,)), dma, dma((NCH, LEVELS)), dma, dma((NCH, LEVELS)),
        dma, dma((n,)), dma, dma((n,)), dma, dma((n,)),
        dma, dma((NCH,)), dma, dma((NCH,)), dma, dma((NCH,)),
        dma, dma((NCH,)), dma, dma((NCH,)), dma, dma((NCH,)), dma, dma((NCH,)),
    ]
    in_vmem = pl.BlockSpec(memory_space=pltpu.VMEM)
    in_any = pl.BlockSpec(memory_space=pl.ANY)
    shapes = (
        jax.ShapeDtypeStruct((LEVELS, 64, D), F32),
        jax.ShapeDtypeStruct((2, 4, 4, 24, D), F32),
        jax.ShapeDtypeStruct((TOK, D), F32),
    )
    outs = pl.pallas_call(
        kernel,
        out_shape=tuple(pltpu.VMEM(o.shape, F32) for o in shapes),
        in_specs=[in_any, in_any, in_any, in_vmem],
        out_specs=(in_vmem,) * 3,
        scratch_shapes=scratch,
        compiler_params=pltpu.CompilerParams(
            collective_id=0, has_side_effects=True, vmem_limit_bytes=58 * 2**20
        ),
        cost_estimate=pl.CostEstimate(flops=13 * 10**9, bytes_accessed=16 * 10**6, transcendentals=0),
        name="quantizer_step",
    )(hidden, enc_weight, codebook, codes)
    code_grad, enc_grad, last = outs
    return code_grad[:, None], enc_grad.reshape(D, D), last


def solution(mesh):
    in_specs = (P(("items", "book"), None), P(), P(None, "book", None), P(None, ("items", "book")))
    out_specs = (P(None, "book", "items", None), P(), P(("items", "book"), None))
    return jax.shard_map(
        on_device, mesh=mesh, in_specs=in_specs, out_specs=out_specs, check_vma=False
    )
```

```python
import jax
import jax.numpy as jnp
from jax import lax
from jax.experimental import pallas as pl
from jax.experimental.pallas import tpu as pltpu
from jax.sharding import PartitionSpec as P

MESH = pl.DeviceIdType.MESH
F32 = jnp.float32
BF16 = jnp.bfloat16
I32 = jnp.int32

TOK = 256
D = 768
LEVELS = 3
SHARD = 2048
CAP = 128
SLOTS = 4 * CAP
CW = 256
NCH = D // CW
UNITS = [(ch, l) for ch in range(NCH) for l in (2, 1, 0)]
RING = 6
MERGED = 9


def onehot(mask):
    return jnp.where(mask, 1.0, 0.0).astype(BF16)


def dot(a, b):
    return jnp.dot(a, b, preferred_element_type=F32)


def iota(shape, axis):
    return lax.broadcasted_iota(I32, shape, axis)


def kernel(
    hid_hbm, w_hbm, cb_hbm, codes, cg_out, enc_out, res_out,
    hid, w, cb, code8, pk, rc, rcs, ut, u, oh, fs, rr, gs, gr, gsib, dd,
    fars, farr, nears, nearr, s2s, s2r, e, ec, e1r, e2s, e2r, ey,
    in_sem, cb_sem, pk_ss, pk_rs, rcs_ss, rcs_rs, f_ss, f_rs, g_ss, g_rs, sib_ss, sib_rs,
    far_ss, far_rs, near_ss, near_rs, s2_ss, s2_rs, h_ss, h_rs, m_ss, ec_ss, ec_rs, e1_ss, e1_rs, e2_ss, e2_rs,
    ey_ss, ey_rs, a1_ss, a1_rs, a2_ss, a2_rs, a3_ss, a3_rs,
):
    i = lax.axis_index("items")
    y = lax.axis_index("book")
    c = i % 2
    x = (i // 2) % 4
    z = i // 8

    def at_y(k):
        return (i, (y + k) % 4)

    def at_x(k):
        return (z * 8 + ((x + k) % 4) * 2 + c, y)

    def at_z(k):
        return (((z + k) % 4) * 8 + x * 2 + c, y)

    sib = (z * 8 + x * 2 + (1 - c), y)

    def remote(src, dst, ss, rs, dev):
        return pltpu.make_async_remote_copy(
            src_ref=src, dst_ref=dst, send_sem=ss, recv_sem=rs, device_id=dev, device_id_type=MESH
        )

    def start(cps):
        for cp in cps:
            cp.start()
        return cps

    def wait(cps):
        for cp in cps:
            cp.wait()

    def took(ref, sem):
        pltpu.make_async_copy(ref, ref, sem).wait()

    bar = pltpu.get_barrier_semaphore()
    for k in (1, 2, 3):
        pl.semaphore_signal(bar, inc=1, device_id=at_y(k), device_id_type=MESH)
        pl.semaphore_signal(bar, inc=1, device_id=at_x(k), device_id_type=MESH)
        pl.semaphore_signal(bar, inc=1, device_id=at_z(k), device_id_type=MESH)
    pl.semaphore_signal(bar, inc=1, device_id=sib, device_id_type=MESH)
    cb_cp = start([
        pltpu.make_async_copy(cb_hbm.at[l], cb.at[l], cb_sem.at[l]) for l in range(LEVELS)
    ])
    in_cp = start([
        pltpu.make_async_copy(hid_hbm, hid, in_sem.at[0]),
        pltpu.make_async_copy(w_hbm, w, in_sem.at[1]),
    ])

    code8[...] = jnp.zeros_like(code8)
    code8[0:LEVELS, :] = codes[...]
    cv = code8[...]
    dist = ((cv >> 11) - y) & 3
    val = (cv & (SHARD - 1)) + 1
    tri = onehot(iota((TOK, TOK), 0) < iota((TOK, TOK), 1))
    pos = jnp.zeros((8, TOK), F32)
    for k in range(4):
        m = jnp.where(dist == k, 1.0, 0.0)
        pos = pos + m * (k * CAP + dot(m.astype(BF16), tri))
    pos_i = pos.astype(I32)
    pos_t = pos.T.astype(I32)
    hl = jnp.concatenate([(val >> 6).astype(F32), (val & 63).astype(F32)], axis=0).astype(BF16)
    pk[...] = jnp.zeros_like(pk)
    for l in range(LEVELS):
        ul = onehot(iota((TOK, SLOTS), 1) == pos_t[:, l : l + 1])
        u[l] = ul
        pc = dot(hl, ul)
        row = pc[l : l + 1, :] * 64.0 + pc[8 + l : 9 + l, :]
        for k in range(4):
            pk[k, l : l + 1, :] = row[:, k * CAP : (k + 1) * CAP]
    rc[0] = pk[0]

    pl.semaphore_wait(bar, 10)
    start([
        remote(pk.at[k], rc.at[4 - k], pk_ss, pk_rs, at_y(k)) for k in (2, 1, 3)
    ])
    for l in range(LEVELS):
        ut[l] = onehot(iota((SLOTS, TOK), 0) == pos_i[l : l + 1, :])
    took(rc.at[1:4], pk_rs)
    remote(rc, rcs, rcs_ss, rcs_rs, sib).start()

    held = jnp.concatenate([rc[k] for k in range(4)], axis=1)
    held_t = held.T.astype(I32)

    def fetch_copies(ch, l):
        return [
            remote(
                fs.at[ch, l, k - 1], rr.at[ch, l, 4 - k],
                f_ss, f_rs.at[NCH + l if ch == 0 and l < 2 else ch], at_y(k),
            )
            for k in (2, 1, 3)
        ]

    def fetch(ch, l):
        cols = slice(ch * CW, (ch + 1) * CW)
        got = dot(oh[l, 0:SLOTS, :], cb[l, 0:1024, cols])
        got = got + dot(oh[l, SLOTS:, :], cb[l, 1024:2048, cols])
        got = got.astype(BF16)
        rr[ch, l, 0] = got[0:CAP]
        for k in (1, 2, 3):
            fs[ch, l, k - 1] = got[k * CAP : (k + 1) * CAP]

    for l in range(LEVELS):
        col = held_t[:, l : l + 1]
        for h in range(2):
            oh[l, h * SLOTS : (h + 1) * SLOTS, :] = onehot(
                iota((SLOTS, 1024), 1) + (1 + h * 1024) == col
            )
        cb_cp[l].wait()
        fetch(0, l)
        start(fetch_copies(0, l))
    for ch in (1, 2):
        for l in range(LEVELS):
            fetch(ch, l)
    wait(in_cp)
    took(rr.at[0, 0, 1:4], f_rs.at[NCH])
    for l in range(LEVELS):
        start(fetch_copies(1, l))

    def chain(ch):
        cols = slice(ch * CW, (ch + 1) * CW)
        if ch == 0:
            took(rr.at[0, 1, 1:4], f_rs.at[NCH + 1])
            took(rr.at[0, 2, 1:4], f_rs.at[0])
        else:
            took(rr.at[ch, :, 1:4], f_rs.at[ch])
        r = dot(hid[...], w[:, cols])
        res = []
        for l in range(LEVELS):
            r = r - dot(u[l], rr[ch, l].reshape(SLOTS, CW))
            res.append(r)
        carried = jnp.zeros_like(r)
        for l in reversed(range(LEVELS)):
            carried = carried + res[l]
            cl = carried.astype(BF16)
            packed = dot(ut[l], cl).astype(BF16)
            gr[ch, l, 0] = packed[0:CAP]
            for k in (1, 2, 3):
                gs[ch, l, k - 1] = packed[k * CAP : (k + 1) * CAP]
            start([
                remote(
                    gs.at[ch, l, k - 1], gr.at[ch, l, 4 - k],
                    g_ss, g_rs.at[ch, l], at_y(k),
                )
                for k in (2, 1, 3)
            ])
            if (ch, l) == (1, 1):
                for fl in range(LEVELS):
                    start(fetch_copies(2, fl))
        res_out[:, cols] = r
        prod = lax.dot_general(
            hid[...], cl, (((0,), (0,)), ((), ())), preferred_element_type=F32
        )
        e[ch] = prod.reshape(2, 4, 4, 24, CW)
        remote(e.at[ch, 1 - c], ec.at[ch], ec_ss, ec_rs.at[ch], sib).start()

    HW = CW // 2

    def enc_b(ch):
        took(ec.at[ch], ec_rs.at[ch])
        e[ch, c] = e[ch, c] + ec[ch]
        cps = []
        for k in (2, 1, 3):
            cps.append(remote(
                e.at[ch, c, :, (x + k) % 4, :, 0:HW], e1r.at[ch, 0, k - 1],
                e1_ss, e1_rs.at[ch], at_x(k),
            ))
            cps.append(remote(
                e.at[ch, c, (z + k) % 4, :, :, HW:CW], e1r.at[ch, 1, k - 1],
                e1_ss, e1_rs.at[ch], at_z(k),
            ))
        start(cps)

    def enc_c(ch):
        took(e1r.at[ch], e1_rs.at[ch])
        t0 = e[ch, c, :, x, :, 0:HW]
        t1 = e[ch, c, z, :, :, HW:CW]
        for k in range(3):
            t0 = t0 + e1r[ch, 0, k]
            t1 = t1 + e1r[ch, 1, k]
        e2s[ch, 0] = t0
        e2s[ch, 1] = t1
        cps = []
        for k in (2, 1, 3):
            cps.append(remote(
                e2s.at[ch, 0, (z + k) % 4], e2r.at[ch, 0, k - 1],
                e2_ss, e2_rs.at[ch], at_z(k),
            ))
            cps.append(remote(
                e2s.at[ch, 1, (x + k) % 4], e2r.at[ch, 1, k - 1],
                e2_ss, e2_rs.at[ch], at_x(k),
            ))
        start(cps)

    def enc_d(ch):
        took(e2r.at[ch], e2_rs.at[ch])
        t0 = e2s[ch, 0, z]
        t1 = e2s[ch, 1, x]
        for k in range(3):
            t0 = t0 + e2r[ch, 0, k]
            t1 = t1 + e2r[ch, 1, k]
        ey[ch, y, :, 0:HW] = t0
        ey[ch, y, :, HW:CW] = t1
        start([
            remote(ey.at[ch, y], ey.at[ch, y], ey_ss, ey_rs.at[ch], at_y(k)) for k in (2, 1, 3)
        ])

    def gather(ch, turn, ss, rs):
        lo = slice(ch * CW, ch * CW + HW)
        hi = slice(ch * CW + HW, (ch + 1) * CW)
        cps = []
        for k in (2, 1, 3):
            if turn == 1:
                va = enc_out.at[c, z, x, :, lo]
                vb = enc_out.at[c, z, x, :, hi]
                da, db = at_x(k), at_z(k)
            else:
                va = enc_out.at[c, z, :, :, lo]
                vb = enc_out.at[c, :, x, :, hi]
                da, db = at_z(k), at_x(k)
            cps.append(remote(va, va, ss, rs.at[ch], da))
            cps.append(remote(vb, vb, ss, rs.at[ch], db))
        start(cps)

    def enc_e(ch):
        took(ey.at[ch, 0:3], ey_rs.at[ch])
        total = ((ey[ch, 0] + ey[ch, 1]) + ey[ch, 2]) + ey[ch, 3]
        enc_out[c, z, x, :, ch * CW : (ch + 1) * CW] = total * (1.0 / (TOK * 128))
        gather(ch, 1, a1_ss, a1_rs)

    def enc_f(ch):
        took(ey.at[ch, 0:3], a1_rs.at[ch])
        gather(ch, 2, a2_ss, a2_rs)

    def enc_g(ch):
        took(ec.at[ch, 0:3], a2_rs.at[ch])
        part = enc_out.at[c, :, :, :, ch * CW : (ch + 1) * CW]
        remote(part, part, a3_ss, a3_rs.at[ch], sib).start()

    def enc_h(ch):
        cols = slice(ch * CW, (ch + 1) * CW)
        took(enc_out.at[1 - c, :, :, :, cols], a3_rs.at[ch])


    def unit_a(n):
        ch, l = UNITS[n]
        took(gr.at[ch, l, 1:4], g_rs.at[ch, l])
        remote(gr.at[ch, l], gsib.at[ch, l], sib_ss, sib_rs.at[ch, l], sib).start()

    def unit_b(n):
        ch, l = UNITS[n]
        q = n % RING
        acc = dot(oh[l, :, 0:SLOTS], gr[ch, l].reshape(SLOTS, CW))
        took(gsib.at[ch, l], sib_rs.at[ch, l])
        acc = acc + dot(oh[l, :, SLOTS:], gsib[ch, l].reshape(SLOTS, CW))
        dd[q] = acc.reshape(4, 4, 64, CW)
        x2 = (x + 2) % 4
        z2 = (z + 2) % 4
        cps = []
        for d, k in enumerate((1, 3)):
            fars[n, 0, d] = dd[q, 2 * d : 2 * d + 2, x2, 0:32, :].astype(BF16)
            fars[n, 1, d] = dd[q, z2, 2 * d : 2 * d + 2, 32:64, :].astype(BF16)
            for h, at in enumerate((at_x, at_z)):
                cps.append(remote(
                    fars.at[n, h, d], farr.at[n, h, d],
                    far_ss, far_rs.at[n], at(k),
                ))
        start(cps)

    def unit_c(n):
        q = n % RING
        took(farr.at[n], far_rs.at[n])
        cps = []
        for d, k in enumerate((1, 3)):
            xk = (x + k) % 4
            zk = (z + k) % 4
            a, b = 2 * d, 2 - 2 * d
            nears[n, 0, d, a : a + 2] = (
                dd[q, a : a + 2, xk, 0:32, :] + farr[n, 0, d].astype(F32)
            ).astype(BF16)
            nears[n, 0, d, b : b + 2] = dd[q, b : b + 2, xk, 0:32, :].astype(BF16)
            nears[n, 1, d, a : a + 2] = (
                dd[q, zk, a : a + 2, 32:64, :] + farr[n, 1, d].astype(F32)
            ).astype(BF16)
            nears[n, 1, d, b : b + 2] = dd[q, zk, b : b + 2, 32:64, :].astype(BF16)
            for h, at in enumerate((at_x, at_z)):
                cps.append(remote(
                    nears.at[n, h, d], nearr.at[n, h, d],
                    near_ss, near_rs.at[n], at(k),
                ))
        start(cps)

    def unit_d(n):
        q = n % RING
        took(nearr.at[n], near_rs.at[n])
        tx = dd[q, :, x, 0:32, :]
        tz = dd[q, z, :, 32:64, :]
        for d in range(2):
            tx = tx + nearr[n, 0, d].astype(F32)
            tz = tz + nearr[n, 1, d].astype(F32)
        s2s[n, 0] = tx
        s2s[n, 1] = tz
        cps = []
        if n < MERGED:
            for d, k in enumerate((1, 3)):
                rows = pl.ds(16 * d, 16)
                cps.append(remote(
                    s2s.at[n, 0, (z + 2) % 4, rows], s2r.at[n, 0, 2, rows], h_ss, h_rs.at[n], at_z(k),
                ))
                cps.append(remote(
                    s2s.at[n, 1, (x + 2) % 4, rows], s2r.at[n, 1, 2, rows], h_ss, h_rs.at[n], at_x(k),
                ))
            start(cps)
            return
        for k in (2, 1, 3):
            cps.append(remote(
                s2s.at[n, 0, (z + k) % 4], s2r.at[n, 0, k - 1],
                s2_ss, s2_rs.at[n], at_z(k),
            ))
            cps.append(remote(
                s2s.at[n, 1, (x + k) % 4], s2r.at[n, 1, k - 1],
                s2_ss, s2_rs.at[n], at_x(k),
            ))
        start(cps)

    def unit_m(n):
        took(s2r.at[n, :, 2], h_rs.at[n])
        cps = []
        for d, k in enumerate((1, 3)):
            rows = slice(16 * d, 16 * d + 16)
            zk = (z + k) % 4
            xk = (x + k) % 4
            s2s[n, 0, zk, rows] = s2s[n, 0, zk, rows] + s2r[n, 0, 2, rows]
            s2s[n, 1, xk, rows] = s2s[n, 1, xk, rows] + s2r[n, 1, 2, rows]
            cps.append(remote(s2s.at[n, 0, zk], s2r.at[n, 0, d], m_ss, s2_rs.at[n], at_z(k)))
            cps.append(remote(s2s.at[n, 1, xk], s2r.at[n, 1, d], m_ss, s2_rs.at[n], at_x(k)))
        start(cps)

    def unit_e(n):
        ch, l = UNITS[n]
        cols = slice(ch * CW, (ch + 1) * CW)
        parts = 2 if n < MERGED else 3
        took(s2r.at[n, :, 0:parts], s2_rs.at[n])
        t0 = s2s[n, 0, z]
        t1 = s2s[n, 1, x]
        for k in range(parts):
            t0 = t0 + s2r[n, 0, k]
            t1 = t1 + s2r[n, 1, k]
        cg_out[l, 0:32, cols] = -t0
        cg_out[l, 32:64, cols] = -t1

    def own_codes():
        took(rcs, rcs_rs)
        for l in range(LEVELS):
            for h, src in enumerate((rc, rcs)):
                slot_code = jnp.concatenate(
                    [src[k, l : l + 1, :] for k in range(4)], axis=1
                ).astype(I32)
                rows = iota((1024, SLOTS), 0)
                code = ((rows >> 6) << 7) + c * 64 + (rows & 63) + 1
                oh[l, :, h * SLOTS : (h + 1) * SLOTS] = onehot(code == slot_code)

    own_codes()
    chain(0)
    enc_b(0)
    chain(1)
    enc_c(0)
    unit_a(0)
    enc_b(1)
    unit_b(0)
    unit_a(1)
    enc_d(0)
    unit_b(1)
    unit_a(2)
    enc_c(1)
    unit_c(0)
    unit_b(2)
    unit_a(3)
    unit_c(1)
    unit_b(3)
    unit_d(0)
    unit_a(4)
    unit_c(2)
    enc_d(1)
    unit_b(4)
    unit_c(3)
    unit_m(0)
    unit_d(1)
    unit_d(2)
    unit_c(4)
    unit_d(3)
    unit_e(0)
    unit_m(1)
    chain(2)
    unit_m(2)
    unit_m(3)
    unit_d(4)
    unit_a(5)
    unit_e(1)
    enc_b(2)
    enc_e(0)
    unit_b(5)
    unit_e(2)
    unit_e(3)
    unit_m(4)
    enc_e(1)
    unit_a(6)
    enc_c(2)
    enc_f(0)
    unit_b(6)
    unit_a(7)
    enc_f(1)
    unit_e(4)
    unit_c(5)
    unit_b(7)
    enc_d(2)
    unit_a(8)
    enc_g(0)
    unit_b(8)
    unit_c(6)
    enc_h(0)
    enc_g(1)
    enc_e(2)
    unit_d(5)
    unit_c(7)
    enc_h(1)
    unit_c(8)
    unit_d(6)
    enc_f(2)
    unit_m(5)
    unit_d(7)
    unit_d(8)
    unit_m(6)
    enc_g(2)
    unit_m(7)
    unit_m(8)
    unit_e(5)
    unit_e(6)
    enc_h(2)
    unit_e(7)
    unit_e(8)
    for ref, sem in (
        (pk.at[1:4], pk_ss), (rc, rcs_ss), (fs, f_ss), (gs, g_ss), (gr, sib_ss), (fars, far_ss),
        (nears, near_ss), (s2r.at[0:MERGED, :, 2], h_ss), (s2r.at[0:MERGED, :, 0:2], m_ss),
         (ec, ec_ss), (e1r, e1_ss), (e2r, e2_ss), (ey.at[:, 0:3], ey_ss),
        (ey.at[:, 0:3], a1_ss), (ec.at[:, 0:3], a2_ss), (ec, a3_ss),
    ):
        took(ref, sem)


def store(a, b, c, ao, bo, co, sem):
    cps = [pltpu.make_async_copy(b.at[k], bo.at[k], sem.at[k]) for k in range(2)]
    cps += [pltpu.make_async_copy(a, ao, sem.at[2]), pltpu.make_async_copy(c, co, sem.at[3])]
    for cp in cps:
        cp.start()
    for cp in cps:
        cp.wait()


def on_device(hidden, enc_weight, codebook, codes):
    dma = pltpu.SemaphoreType.DMA
    vmem = pltpu.VMEM
    n = len(UNITS)
    scratch = [
        vmem((TOK, D), BF16),
        vmem((D, D), BF16),
        vmem((LEVELS, SHARD, D), BF16),
        vmem((8, TOK), I32),
        vmem((4, 8, CAP), F32),
        vmem((4, 8, CAP), F32),
        vmem((4, 8, CAP), F32),
        vmem((LEVELS, SLOTS, TOK), BF16),
        vmem((LEVELS, TOK, SLOTS), BF16),
        vmem((LEVELS, 1024, 1024), BF16),
        vmem((NCH, LEVELS, 3, CAP, CW), BF16),
        vmem((NCH, LEVELS, 4, CAP, CW), BF16),
        vmem((NCH, LEVELS, 3, CAP, CW), BF16),
        vmem((NCH, LEVELS, 4, CAP, CW), BF16),
        vmem((NCH, LEVELS, 4, CAP, CW), BF16),
        vmem((RING, 4, 4, 64, CW), F32),
        vmem((n, 2, 2, 2, 32, CW), BF16),
        vmem((n, 2, 2, 2, 32, CW), BF16),
        vmem((n, 2, 2, 4, 32, CW), BF16),
        vmem((n, 2, 2, 4, 32, CW), BF16),
        vmem((n, 2, 4, 32, CW), F32),
        vmem((n, 2, 3, 32, CW), F32),
        vmem((NCH, 2, 4, 4, 24, CW), F32),
        vmem((NCH, 4, 4, 24, CW), F32),
        vmem((NCH, 2, 3, 4, 24, CW // 2), F32),
        vmem((NCH, 2, 4, 24, CW // 2), F32),
        vmem((NCH, 2, 3, 24, CW // 2), F32),
        vmem((NCH, 4, 24, CW), F32),
        dma((2,)), dma((LEVELS,)),
        dma, dma, dma, dma,
        dma, dma((NCH + 2,)), dma, dma((NCH, LEVELS)), dma, dma((NCH, LEVELS)),
        dma, dma((n,)), dma, dma((n,)), dma, dma((n,)), dma, dma((n,)), dma,
        dma, dma((NCH,)), dma, dma((NCH,)), dma, dma((NCH,)),
        dma, dma((NCH,)), dma, dma((NCH,)), dma, dma((NCH,)), dma, dma((NCH,)),
    ]
    in_vmem = pl.BlockSpec(memory_space=pltpu.VMEM)
    in_any = pl.BlockSpec(memory_space=pl.ANY)
    shapes = (
        jax.ShapeDtypeStruct((LEVELS, 64, D), F32),
        jax.ShapeDtypeStruct((2, 4, 4, 24, D), F32),
        jax.ShapeDtypeStruct((TOK, D), F32),
    )
    outs = pl.pallas_call(
        kernel,
        out_shape=tuple(pltpu.VMEM(o.shape, F32) for o in shapes),
        in_specs=[in_any, in_any, in_any, in_vmem],
        out_specs=(in_vmem,) * 3,
        scratch_shapes=scratch,
        compiler_params=pltpu.CompilerParams(
            collective_id=0, has_side_effects=True, vmem_limit_bytes=58 * 2**20
        ),
        cost_estimate=pl.CostEstimate(flops=13 * 10**9, bytes_accessed=16 * 10**6, transcendentals=0),
        name="quantizer_step",
    )(hidden, enc_weight, codebook, codes)
    code_grad, enc_grad, last = outs
    return code_grad[:, None], enc_grad.reshape(D, D), last


def solution(mesh):
    in_specs = (P(("items", "book"), None), P(), P(None, "book", None), P(None, ("items", "book")))
    out_specs = (P(None, "book", "items", None), P(), P(("items", "book"), None))
    return jax.shard_map(
        on_device, mesh=mesh, in_specs=in_specs, out_specs=out_specs, check_vma=False
    )
```

```python
import jax
import jax.numpy as jnp
from jax import lax
from jax.experimental import pallas as pl
from jax.experimental.pallas import tpu as pltpu
from jax.sharding import PartitionSpec as P

MESH = pl.DeviceIdType.MESH
F32 = jnp.float32
BF16 = jnp.bfloat16
I32 = jnp.int32

TOK = 256
D = 768
LEVELS = 3
SHARD = 2048
CAP = 128
SLOTS = 4 * CAP
CW = 256
NCH = D // CW
UNITS = [(ch, l) for ch in range(NCH) for l in (2, 1, 0)]
RING = 6
MERGED = 9


def onehot(mask):
    return jnp.where(mask, 1.0, 0.0).astype(BF16)


def dot(a, b):
    return jnp.dot(a, b, preferred_element_type=F32)


def iota(shape, axis):
    return lax.broadcasted_iota(I32, shape, axis)


def kernel(
    hid_hbm, w_hbm, cb_hbm, codes, cg_out, enc_out, res_out,
    hid, w, cb, code8, pk, rc, rcs, ut, u, oh, fs, rr, gs, gr, gsib, dd,
    fars, farr, nears, nearr, s2s, s2r, e, ec, e1r, e2s, e2r, ey,
    in_sem, cb_sem, pk_ss, pk_rs, rcs_ss, rcs_rs, f_ss, f_rs, g_ss, g_rs, sib_ss, sib_rs,
    far_ss, far_rs, near_ss, near_rs, s2_ss, s2_rs, h_ss, h_rs, m_ss, ec_ss, ec_rs, e1_ss, e1_rs, e2_ss, e2_rs,
    ey_ss, ey_rs, a1_ss, a1_rs, a2_ss, a2_rs, a3_ss, a3_rs,
):
    i = lax.axis_index("items")
    y = lax.axis_index("book")
    c = i % 2
    x = (i // 2) % 4
    z = i // 8

    def at_y(k):
        return (i, (y + k) % 4)

    def at_x(k):
        return (z * 8 + ((x + k) % 4) * 2 + c, y)

    def at_z(k):
        return (((z + k) % 4) * 8 + x * 2 + c, y)

    sib = (z * 8 + x * 2 + (1 - c), y)

    def remote(src, dst, ss, rs, dev):
        return pltpu.make_async_remote_copy(
            src_ref=src, dst_ref=dst, send_sem=ss, recv_sem=rs, device_id=dev, device_id_type=MESH
        )

    def start(cps):
        for cp in cps:
            cp.start()
        return cps

    def wait(cps):
        for cp in cps:
            cp.wait()

    def took(ref, sem):
        pltpu.make_async_copy(ref, ref, sem).wait()

    bar = pltpu.get_barrier_semaphore()
    for k in (1, 2, 3):
        pl.semaphore_signal(bar, inc=1, device_id=at_y(k), device_id_type=MESH)
        pl.semaphore_signal(bar, inc=1, device_id=at_x(k), device_id_type=MESH)
        pl.semaphore_signal(bar, inc=1, device_id=at_z(k), device_id_type=MESH)
    pl.semaphore_signal(bar, inc=1, device_id=sib, device_id_type=MESH)
    cb_cp = start([
        pltpu.make_async_copy(cb_hbm.at[l], cb.at[l], cb_sem.at[l]) for l in range(LEVELS)
    ])
    in_cp = start([
        pltpu.make_async_copy(hid_hbm, hid, in_sem.at[0]),
        pltpu.make_async_copy(w_hbm, w, in_sem.at[1]),
    ])

    code8[...] = jnp.zeros_like(code8)
    code8[0:LEVELS, :] = codes[...]
    cv = code8[...]
    dist = ((cv >> 11) - y) & 3
    val = (cv & (SHARD - 1)) + 1
    tri = onehot(iota((TOK, TOK), 0) < iota((TOK, TOK), 1))
    pos = jnp.zeros((8, TOK), F32)
    for k in range(4):
        m = jnp.where(dist == k, 1.0, 0.0)
        pos = pos + m * (k * CAP + dot(m.astype(BF16), tri))
    pos_i = pos.astype(I32)
    pos_t = pos.T.astype(I32)
    hl = jnp.concatenate([(val >> 6).astype(F32), (val & 63).astype(F32)], axis=0).astype(BF16)
    pk[...] = jnp.zeros_like(pk)
    for l in range(LEVELS):
        ul = onehot(iota((TOK, SLOTS), 1) == pos_t[:, l : l + 1])
        u[l] = ul
        pc = dot(hl, ul)
        row = pc[l : l + 1, :] * 64.0 + pc[8 + l : 9 + l, :]
        for k in range(4):
            pk[k, l : l + 1, :] = row[:, k * CAP : (k + 1) * CAP]
    rc[0] = pk[0]

    pl.semaphore_wait(bar, 10)
    start([
        remote(pk.at[k], rc.at[4 - k], pk_ss, pk_rs, at_y(k)) for k in (2, 1, 3)
    ])
    for l in range(LEVELS):
        ut[l] = onehot(iota((SLOTS, TOK), 0) == pos_i[l : l + 1, :])
    took(rc.at[1:4], pk_rs)
    remote(rc, rcs, rcs_ss, rcs_rs, sib).start()

    held = jnp.concatenate([rc[k] for k in range(4)], axis=1)
    held_t = held.T.astype(I32)

    def fetch_copies(ch, l):
        return [
            remote(
                fs.at[ch, l, k - 1], rr.at[ch, l, 4 - k],
                f_ss, f_rs.at[NCH + l if ch == 0 and l < 2 else ch], at_y(k),
            )
            for k in (2, 1, 3)
        ]

    def fetch(ch, l):
        cols = slice(ch * CW, (ch + 1) * CW)
        got = dot(oh[l, 0:SLOTS, :], cb[l, 0:1024, cols])
        got = got + dot(oh[l, SLOTS:, :], cb[l, 1024:2048, cols])
        got = got.astype(BF16)
        rr[ch, l, 0] = got[0:CAP]
        for k in (1, 2, 3):
            fs[ch, l, k - 1] = got[k * CAP : (k + 1) * CAP]

    for l in range(LEVELS):
        col = held_t[:, l : l + 1]
        for h in range(2):
            oh[l, h * SLOTS : (h + 1) * SLOTS, :] = onehot(
                iota((SLOTS, 1024), 1) + (1 + h * 1024) == col
            )
        cb_cp[l].wait()
        fetch(0, l)
        start(fetch_copies(0, l))
    for ch in (1, 2):
        for l in range(LEVELS):
            fetch(ch, l)
    wait(in_cp)
    took(rr.at[0, 0, 1:4], f_rs.at[NCH])

    def fetch_rest(ch):
        start([
            remote(fs.at[ch, :, k - 1], rr.at[ch, :, 4 - k], f_ss, f_rs.at[ch], at_y(k))
            for k in (2, 1, 3)
        ])

    fetch_rest(1)

    def chain(ch):
        cols = slice(ch * CW, (ch + 1) * CW)
        if ch == 0:
            took(rr.at[0, 1, 1:4], f_rs.at[NCH + 1])
            took(rr.at[0, 2, 1:4], f_rs.at[0])
        else:
            took(rr.at[ch, :, 1:4], f_rs.at[ch])
        r = dot(hid[...], w[:, cols])
        res = []
        for l in range(LEVELS):
            r = r - dot(u[l], rr[ch, l].reshape(SLOTS, CW))
            res.append(r)
        carried = jnp.zeros_like(r)
        for l in reversed(range(LEVELS)):
            carried = carried + res[l]
            cl = carried.astype(BF16)
            packed = dot(ut[l], cl).astype(BF16)
            gr[ch, l, 0] = packed[0:CAP]
            for k in (1, 2, 3):
                gs[ch, l, k - 1] = packed[k * CAP : (k + 1) * CAP]
            start([
                remote(
                    gs.at[ch, l, k - 1], gr.at[ch, l, 4 - k],
                    g_ss, g_rs.at[ch, l], at_y(k),
                )
                for k in (2, 1, 3)
            ])
            if (ch, l) == (1, 1):
                fetch_rest(2)
        res_out[:, cols] = r
        prod = lax.dot_general(
            hid[...], cl, (((0,), (0,)), ((), ())), preferred_element_type=F32
        )
        e[ch] = prod.reshape(2, 4, 4, 24, CW)
        remote(e.at[ch, 1 - c], ec.at[ch], ec_ss, ec_rs.at[ch], sib).start()

    HW = CW // 2

    def enc_b(ch):
        took(ec.at[ch], ec_rs.at[ch])
        e[ch, c] = e[ch, c] + ec[ch]
        cps = []
        for k in (2, 1, 3):
            cps.append(remote(
                e.at[ch, c, :, (x + k) % 4, :, 0:HW], e1r.at[ch, 0, k - 1],
                e1_ss, e1_rs.at[ch], at_x(k),
            ))
            cps.append(remote(
                e.at[ch, c, (z + k) % 4, :, :, HW:CW], e1r.at[ch, 1, k - 1],
                e1_ss, e1_rs.at[ch], at_z(k),
            ))
        start(cps)

    def enc_c(ch):
        took(e1r.at[ch], e1_rs.at[ch])
        t0 = e[ch, c, :, x, :, 0:HW]
        t1 = e[ch, c, z, :, :, HW:CW]
        for k in range(3):
            t0 = t0 + e1r[ch, 0, k]
            t1 = t1 + e1r[ch, 1, k]
        e2s[ch, 0] = t0
        e2s[ch, 1] = t1
        cps = []
        for k in (2, 1, 3):
            cps.append(remote(
                e2s.at[ch, 0, (z + k) % 4], e2r.at[ch, 0, k - 1],
                e2_ss, e2_rs.at[ch], at_z(k),
            ))
            cps.append(remote(
                e2s.at[ch, 1, (x + k) % 4], e2r.at[ch, 1, k - 1],
                e2_ss, e2_rs.at[ch], at_x(k),
            ))
        start(cps)

    def enc_d(ch):
        took(e2r.at[ch], e2_rs.at[ch])
        t0 = e2s[ch, 0, z]
        t1 = e2s[ch, 1, x]
        for k in range(3):
            t0 = t0 + e2r[ch, 0, k]
            t1 = t1 + e2r[ch, 1, k]
        ey[ch, y, :, 0:HW] = t0
        ey[ch, y, :, HW:CW] = t1
        start([
            remote(ey.at[ch, y], ey.at[ch, y], ey_ss, ey_rs.at[ch], at_y(k)) for k in (2, 1, 3)
        ])

    def gather(ch, turn, ss, rs):
        lo = slice(ch * CW, ch * CW + HW)
        hi = slice(ch * CW + HW, (ch + 1) * CW)
        cps = []
        for k in (2, 1, 3):
            if turn == 1:
                va = enc_out.at[c, z, x, :, lo]
                vb = enc_out.at[c, z, x, :, hi]
                da, db = at_x(k), at_z(k)
            else:
                va = enc_out.at[c, z, :, :, lo]
                vb = enc_out.at[c, :, x, :, hi]
                da, db = at_z(k), at_x(k)
            cps.append(remote(va, va, ss, rs.at[ch], da))
            cps.append(remote(vb, vb, ss, rs.at[ch], db))
        start(cps)

    def enc_e(ch):
        took(ey.at[ch, 0:3], ey_rs.at[ch])
        total = ((ey[ch, 0] + ey[ch, 1]) + ey[ch, 2]) + ey[ch, 3]
        enc_out[c, z, x, :, ch * CW : (ch + 1) * CW] = total * (1.0 / (TOK * 128))
        gather(ch, 1, a1_ss, a1_rs)

    def enc_f(ch):
        took(ey.at[ch, 0:3], a1_rs.at[ch])
        gather(ch, 2, a2_ss, a2_rs)

    def enc_g(ch):
        took(ec.at[ch, 0:3], a2_rs.at[ch])
        part = enc_out.at[c, :, :, :, ch * CW : (ch + 1) * CW]
        remote(part, part, a3_ss, a3_rs.at[ch], sib).start()

    def enc_h(ch):
        cols = slice(ch * CW, (ch + 1) * CW)
        took(enc_out.at[1 - c, :, :, :, cols], a3_rs.at[ch])


    def unit_a(n):
        ch, l = UNITS[n]
        took(gr.at[ch, l, 1:4], g_rs.at[ch, l])
        remote(gr.at[ch, l], gsib.at[ch, l], sib_ss, sib_rs.at[ch, l], sib).start()

    def unit_b(n):
        ch, l = UNITS[n]
        q = n % RING
        acc = dot(oh[l, :, 0:SLOTS], gr[ch, l].reshape(SLOTS, CW))
        took(gsib.at[ch, l], sib_rs.at[ch, l])
        acc = acc + dot(oh[l, :, SLOTS:], gsib[ch, l].reshape(SLOTS, CW))
        dd[q] = acc.reshape(4, 4, 64, CW)
        x2 = (x + 2) % 4
        z2 = (z + 2) % 4
        cps = []
        for d, k in enumerate((1, 3)):
            fars[n, 0, d] = dd[q, 2 * d : 2 * d + 2, x2, 0:32, :].astype(BF16)
            fars[n, 1, d] = dd[q, z2, 2 * d : 2 * d + 2, 32:64, :].astype(BF16)
            for h, at in enumerate((at_x, at_z)):
                cps.append(remote(
                    fars.at[n, h, d], farr.at[n, h, d],
                    far_ss, far_rs.at[n], at(k),
                ))
        start(cps)

    def unit_c(n):
        q = n % RING
        took(farr.at[n], far_rs.at[n])
        cps = []
        for d, k in enumerate((1, 3)):
            xk = (x + k) % 4
            zk = (z + k) % 4
            a, b = 2 * d, 2 - 2 * d
            nears[n, 0, d, a : a + 2] = (
                dd[q, a : a + 2, xk, 0:32, :] + farr[n, 0, d].astype(F32)
            ).astype(BF16)
            nears[n, 0, d, b : b + 2] = dd[q, b : b + 2, xk, 0:32, :].astype(BF16)
            nears[n, 1, d, a : a + 2] = (
                dd[q, zk, a : a + 2, 32:64, :] + farr[n, 1, d].astype(F32)
            ).astype(BF16)
            nears[n, 1, d, b : b + 2] = dd[q, zk, b : b + 2, 32:64, :].astype(BF16)
            for h, at in enumerate((at_x, at_z)):
                cps.append(remote(
                    nears.at[n, h, d], nearr.at[n, h, d],
                    near_ss, near_rs.at[n], at(k),
                ))
        start(cps)

    def unit_d(n):
        q = n % RING
        took(nearr.at[n], near_rs.at[n])
        tx = dd[q, :, x, 0:32, :]
        tz = dd[q, z, :, 32:64, :]
        for d in range(2):
            tx = tx + nearr[n, 0, d].astype(F32)
            tz = tz + nearr[n, 1, d].astype(F32)
        s2s[n, 0] = tx
        s2s[n, 1] = tz
        cps = []
        if n < MERGED:
            for d, k in enumerate((1, 3)):
                rows = pl.ds(16 * d, 16)
                cps.append(remote(
                    s2s.at[n, 0, (z + 2) % 4, rows], s2r.at[n, 0, 2, rows], h_ss, h_rs.at[n], at_z(k),
                ))
                cps.append(remote(
                    s2s.at[n, 1, (x + 2) % 4, rows], s2r.at[n, 1, 2, rows], h_ss, h_rs.at[n], at_x(k),
                ))
            start(cps)
            return
        for k in (2, 1, 3):
            cps.append(remote(
                s2s.at[n, 0, (z + k) % 4], s2r.at[n, 0, k - 1],
                s2_ss, s2_rs.at[n], at_z(k),
            ))
            cps.append(remote(
                s2s.at[n, 1, (x + k) % 4], s2r.at[n, 1, k - 1],
                s2_ss, s2_rs.at[n], at_x(k),
            ))
        start(cps)

    def unit_m(n):
        took(s2r.at[n, :, 2], h_rs.at[n])
        cps = []
        for d, k in enumerate((1, 3)):
            rows = slice(16 * d, 16 * d + 16)
            zk = (z + k) % 4
            xk = (x + k) % 4
            s2s[n, 0, zk, rows] = s2s[n, 0, zk, rows] + s2r[n, 0, 2, rows]
            s2s[n, 1, xk, rows] = s2s[n, 1, xk, rows] + s2r[n, 1, 2, rows]
            cps.append(remote(s2s.at[n, 0, zk], s2r.at[n, 0, d], m_ss, s2_rs.at[n], at_z(k)))
            cps.append(remote(s2s.at[n, 1, xk], s2r.at[n, 1, d], m_ss, s2_rs.at[n], at_x(k)))
        start(cps)

    def unit_e(n):
        ch, l = UNITS[n]
        cols = slice(ch * CW, (ch + 1) * CW)
        parts = 2 if n < MERGED else 3
        took(s2r.at[n, :, 0:parts], s2_rs.at[n])
        t0 = s2s[n, 0, z]
        t1 = s2s[n, 1, x]
        for k in range(parts):
            t0 = t0 + s2r[n, 0, k]
            t1 = t1 + s2r[n, 1, k]
        cg_out[l, 0:32, cols] = -t0
        cg_out[l, 32:64, cols] = -t1

    def own_codes():
        took(rcs, rcs_rs)
        for l in range(LEVELS):
            for h, src in enumerate((rc, rcs)):
                slot_code = jnp.concatenate(
                    [src[k, l : l + 1, :] for k in range(4)], axis=1
                ).astype(I32)
                rows = iota((1024, SLOTS), 0)
                code = ((rows >> 6) << 7) + c * 64 + (rows & 63) + 1
                oh[l, :, h * SLOTS : (h + 1) * SLOTS] = onehot(code == slot_code)

    own_codes()
    chain(0)
    enc_b(0)
    chain(1)
    enc_c(0)
    unit_a(0)
    enc_b(1)
    unit_b(0)
    unit_a(1)
    enc_d(0)
    unit_b(1)
    unit_a(2)
    enc_c(1)
    unit_c(0)
    unit_b(2)
    unit_a(3)
    unit_c(1)
    unit_b(3)
    unit_d(0)
    unit_a(4)
    unit_c(2)
    enc_d(1)
    unit_b(4)
    unit_c(3)
    unit_m(0)
    unit_d(1)
    unit_d(2)
    unit_c(4)
    unit_d(3)
    unit_e(0)
    unit_m(1)
    chain(2)
    unit_m(2)
    unit_m(3)
    unit_d(4)
    unit_a(5)
    unit_e(1)
    enc_b(2)
    enc_e(0)
    unit_b(5)
    unit_e(2)
    unit_e(3)
    unit_m(4)
    enc_e(1)
    unit_a(6)
    enc_c(2)
    enc_f(0)
    unit_b(6)
    unit_a(7)
    enc_f(1)
    unit_e(4)
    unit_c(5)
    unit_b(7)
    enc_d(2)
    unit_a(8)
    enc_g(0)
    unit_b(8)
    unit_c(6)
    enc_h(0)
    enc_g(1)
    enc_e(2)
    unit_d(5)
    unit_c(7)
    enc_h(1)
    unit_c(8)
    unit_d(6)
    enc_f(2)
    unit_m(5)
    unit_d(7)
    unit_d(8)
    unit_m(6)
    enc_g(2)
    unit_m(7)
    unit_m(8)
    unit_e(5)
    unit_e(6)
    enc_h(2)
    unit_e(7)
    unit_e(8)
    for ref, sem in (
        (pk.at[1:4], pk_ss), (rc, rcs_ss), (fs, f_ss), (gs, g_ss), (gr, sib_ss), (fars, far_ss),
        (nears, near_ss), (s2r.at[0:MERGED, :, 2], h_ss), (s2r.at[0:MERGED, :, 0:2], m_ss),
         (ec, ec_ss), (e1r, e1_ss), (e2r, e2_ss), (ey.at[:, 0:3], ey_ss),
        (ey.at[:, 0:3], a1_ss), (ec.at[:, 0:3], a2_ss), (ec, a3_ss),
    ):
        took(ref, sem)


def store(a, b, c, ao, bo, co, sem):
    cps = [pltpu.make_async_copy(b.at[k], bo.at[k], sem.at[k]) for k in range(2)]
    cps += [pltpu.make_async_copy(a, ao, sem.at[2]), pltpu.make_async_copy(c, co, sem.at[3])]
    for cp in cps:
        cp.start()
    for cp in cps:
        cp.wait()


def on_device(hidden, enc_weight, codebook, codes):
    dma = pltpu.SemaphoreType.DMA
    vmem = pltpu.VMEM
    n = len(UNITS)
    scratch = [
        vmem((TOK, D), BF16),
        vmem((D, D), BF16),
        vmem((LEVELS, SHARD, D), BF16),
        vmem((8, TOK), I32),
        vmem((4, 8, CAP), F32),
        vmem((4, 8, CAP), F32),
        vmem((4, 8, CAP), F32),
        vmem((LEVELS, SLOTS, TOK), BF16),
        vmem((LEVELS, TOK, SLOTS), BF16),
        vmem((LEVELS, 1024, 1024), BF16),
        vmem((NCH, LEVELS, 3, CAP, CW), BF16),
        vmem((NCH, LEVELS, 4, CAP, CW), BF16),
        vmem((NCH, LEVELS, 3, CAP, CW), BF16),
        vmem((NCH, LEVELS, 4, CAP, CW), BF16),
        vmem((NCH, LEVELS, 4, CAP, CW), BF16),
        vmem((RING, 4, 4, 64, CW), F32),
        vmem((n, 2, 2, 2, 32, CW), BF16),
        vmem((n, 2, 2, 2, 32, CW), BF16),
        vmem((n, 2, 2, 4, 32, CW), BF16),
        vmem((n, 2, 2, 4, 32, CW), BF16),
        vmem((n, 2, 4, 32, CW), F32),
        vmem((n, 2, 3, 32, CW), F32),
        vmem((NCH, 2, 4, 4, 24, CW), F32),
        vmem((NCH, 4, 4, 24, CW), F32),
        vmem((NCH, 2, 3, 4, 24, CW // 2), F32),
        vmem((NCH, 2, 4, 24, CW // 2), F32),
        vmem((NCH, 2, 3, 24, CW // 2), F32),
        vmem((NCH, 4, 24, CW), F32),
        dma((2,)), dma((LEVELS,)),
        dma, dma, dma, dma,
        dma, dma((NCH + 2,)), dma, dma((NCH, LEVELS)), dma, dma((NCH, LEVELS)),
        dma, dma((n,)), dma, dma((n,)), dma, dma((n,)), dma, dma((n,)), dma,
        dma, dma((NCH,)), dma, dma((NCH,)), dma, dma((NCH,)),
        dma, dma((NCH,)), dma, dma((NCH,)), dma, dma((NCH,)), dma, dma((NCH,)),
    ]
    in_vmem = pl.BlockSpec(memory_space=pltpu.VMEM)
    in_any = pl.BlockSpec(memory_space=pl.ANY)
    shapes = (
        jax.ShapeDtypeStruct((LEVELS, 64, D), F32),
        jax.ShapeDtypeStruct((2, 4, 4, 24, D), F32),
        jax.ShapeDtypeStruct((TOK, D), F32),
    )
    outs = pl.pallas_call(
        kernel,
        out_shape=tuple(pltpu.VMEM(o.shape, F32) for o in shapes),
        in_specs=[in_any, in_any, in_any, in_vmem],
        out_specs=(in_vmem,) * 3,
        scratch_shapes=scratch,
        compiler_params=pltpu.CompilerParams(
            collective_id=0, has_side_effects=True, vmem_limit_bytes=58 * 2**20
        ),
        cost_estimate=pl.CostEstimate(flops=13 * 10**9, bytes_accessed=16 * 10**6, transcendentals=0),
        name="quantizer_step",
    )(hidden, enc_weight, codebook, codes)
    code_grad, enc_grad, last = outs
    return code_grad[:, None], enc_grad.reshape(D, D), last


def solution(mesh):
    in_specs = (P(("items", "book"), None), P(), P(None, "book", None), P(None, ("items", "book")))
    out_specs = (P(None, "book", "items", None), P(), P(("items", "book"), None))
    return jax.shard_map(
        on_device, mesh=mesh, in_specs=in_specs, out_specs=out_specs, check_vma=False
    )
```
